256 devices in a mesh: mode: 8 (over x, y_lo), space: 32 (over y_hi, z, core).
Axes of the slice: x: 4, y: 4 (y_hi: 2, y_lo: 2; y = y_hi * 2 + y_lo), z: 8, core: 2. Of those that a mesh axis runs over, the one named last changes fastest.
Arguments:
- basis: float32 [192, 3, 64, 16, 128], P('mode', None, 'space'), may hold values from -6 to 6
- density: float32 [64, 16, 128], P('space'), may hold values from 0.03 to 1
Outputs:
- rotated: float32 [192, 3, 64, 16, 128], P('mode', None, 'space')
- reduced: float32 [192, 192], replicated
The draws below stay inside these ranges and needn't reach their ends.
All inputs are finite; a program needn't handle non-finite values.
Results may differ from the reference program's by a relative error of at most 0.00011.
Values sent between devices are 32-bit elements; how exact they have to be, the bound alone decides.
No kernel may reach another device: no remote copies, remote signals or barrier semaphores. Data moves between devices by JAX's collectives and lax.ppermute only.
A program may use at most 128 MiB of HBM per device.

```python
import math
import jax
import jax.numpy as jnp
import numpy as np
from jax import lax

COLS = 192
NY = 16
NZ = 128
NX = 64


def draw_density(key, part):
    key = jax.random.fold_in(key, 7)
    position = jnp.arange(NX, dtype=jnp.float32)[:, None, None] / (NX - 1.0)
    random_part = jnp.exp(jax.random.uniform(key, (NX, NY, NZ), jnp.float32, math.log(0.1), 0.0))
    return random_part * (1.0 / 3.0 + 2.0 / 3.0 * position)


def block_levels(rng, extent, shards, smallest, largest):
    def one(axis_at, shards_of):
        draws = jax.random.uniform(jax.random.fold_in(jax.random.fold_in(rng, 6), axis_at), (shards_of,), jnp.float32, smallest / len(shards), largest / len(shards))
        return jnp.repeat(jnp.exp(draws), extent[axis_at] // shards_of).reshape((-1,) + (1,) * (len(extent) - axis_at - 1))

    level = one(*shards[0])
    for cut in shards[1:]:
        level = level * one(*cut)
    return level


def gaussian(rng, shape, width, reach, shards=(), held_as=jnp.bfloat16):
    level = block_levels(rng, shape, shards, -0.22, 0.18) if shards else 1.0
    values = jax.random.normal(rng, shape, jnp.float32) * width * level
    return jnp.minimum(jnp.maximum(values, -reach), reach).astype(held_as)


def setup_inputs(seed: int = 0) -> dict:
    seeds = jax.random.split(jax.random.key(seed), 3)
    basis = gaussian(seeds[0], (COLS, 3, NX, NY, NZ), 1.0, 6.0, ((0, 8), (2, 32)), jnp.float32)
    density = draw_density(jax.random.fold_in(seeds[2], 71), 0)
    return dict(basis=basis, density=density)


def hex_tables():
    poisson = 0.3
    lame_first = poisson / ((1.0 + poisson) * (1.0 - 2.0 * poisson))
    shear = 1.0 / (2.0 * (1.0 + poisson))
    elastic = np.zeros((6, 6))
    elastic[:3, :3] = lame_first
    for number in range(3):
        elastic[number, number] += 2.0 * shear
        elastic[number + 3, number + 3] = shear
    points = [0.5 - 0.5 / math.sqrt(3.0), 0.5 + 0.5 / math.sqrt(3.0)]
    corners = [(along_x, along_y, along_z) for along_x in (0, 1) for along_y in (0, 1) for along_z in (0, 1)]
    stiff = np.zeros((24, 24))
    for point_x in points:
        for point_y in points:
            for point_z in points:
                strain = np.zeros((6, 24))
                for number, corner in enumerate(corners):
                    shape_x = point_x if corner[0] else 1.0 - point_x
                    shape_y = point_y if corner[1] else 1.0 - point_y
                    shape_z = point_z if corner[2] else 1.0 - point_z
                    deriv_x = (2.0 * corner[0] - 1.0) * shape_y * shape_z
                    deriv_y = shape_x * (2.0 * corner[1] - 1.0) * shape_z
                    deriv_z = shape_x * shape_y * (2.0 * corner[2] - 1.0)
                    strain[0, 3 * number] = deriv_x
                    strain[1, 3 * number + 1] = deriv_y
                    strain[2, 3 * number + 2] = deriv_z
                    strain[3, 3 * number] = deriv_y
                    strain[3, 3 * number + 1] = deriv_x
                    strain[4, 3 * number + 1] = deriv_z
                    strain[4, 3 * number + 2] = deriv_y
                    strain[5, 3 * number] = deriv_z
                    strain[5, 3 * number + 2] = deriv_x
                stiff += strain.T @ elastic @ strain / 8.0
    nodal = np.zeros((8, 8))
    for first, corner_one in enumerate(corners):
        for second, corner_two in enumerate(corners):
            nodal[first, second] = math.prod([1.0 / 3.0 if corner_one[axis_number] == corner_two[axis_number] else 1.0 / 6.0 for axis_number in range(3)])
    massfull = np.kron(nodal, np.eye(3))
    return np.stack([stiff, massfull]).reshape(2, 8, 3, 8, 3).astype(np.float32)

def element_forces(padded, extended, tables, planes):
    corner_list = []
    for along_x in (0, 1):
        for along_y in (0, 1):
            for along_z in (0, 1):
                piece = padded[:, :, along_x:along_x + planes + 1]
                corner_list.append(jnp.roll(piece, (-along_y, -along_z), axis=(3, 4)))
    stacked = jnp.stack(corner_list)
    forces = jnp.einsum('knpmq,mgqxyz->kngpxyz', tables, stacked, precision=lax.Precision.HIGHEST)
    weights = jnp.stack([extended * extended * extended, extended])
    forces = forces * weights[:, None, None, None]
    total = jnp.zeros((2, padded.shape[0], 3, planes, padded.shape[3], padded.shape[4]), jnp.float32)
    number = 0
    for along_x in (0, 1):
        for along_y in (0, 1):
            for along_z in (0, 1):
                piece = forces[:, number, :, :, 1 - along_x:1 - along_x + planes]
                total = total + jnp.roll(piece, (along_y, along_z), axis=(4, 5))
                number += 1
    return total

def reference(basis, density):
    tables = jnp.asarray(hex_tables())
    extended = jnp.concatenate([jnp.zeros((1, NY, NZ), jnp.float32), density], axis=0)
    groups = basis.reshape(COLS // 4, 4, 3, NX, NY, NZ)

    def apply_group(field):
        padded = jnp.pad(field, ((0, 0), (0, 0), (1, 1), (0, 0), (0, 0)))
        return element_forces(padded, extended, tables, NX)
    applied = lax.map(apply_group, groups)
    applied = jnp.moveaxis(applied, 1, 0).reshape(2, COLS, 3 * NX * NY * NZ)
    flat = basis.reshape(COLS, 3 * NX * NY * NZ)
    scale = 1.0 / (3.0 * NX * NY * NZ)
    gram_stiff = jnp.dot(flat, applied[0].T, precision=lax.Precision.HIGHEST) * scale
    gram_mass = jnp.dot(flat, applied[1].T, precision=lax.Precision.HIGHEST) * scale
    lower = jnp.linalg.cholesky(gram_mass)
    inverse = lax.linalg.triangular_solve(lower, jnp.eye(COLS, dtype=lower.dtype), left_side=True, lower=True)
    reduced = jnp.dot(jnp.dot(inverse, gram_stiff, precision=lax.Precision.HIGHEST), inverse.T, precision=lax.Precision.HIGHEST)
    rotated = jnp.dot(inverse, flat, precision=lax.Precision.HIGHEST).reshape(basis.shape)
    return (rotated, reduced)
```

```python
import functools
import math

import jax
import jax.numpy as jnp
import numpy as np
from jax import lax
from jax.experimental import pallas as pl
from jax.experimental.pallas import tpu as pltpu
from jax.sharding import Mesh, PartitionSpec as P

VMEM = pltpu.VMEM
MODE = ("x", "yl")
SPACE = ("yh", "zc")
F32 = jnp.float32
BF16 = jnp.bfloat16


def hex_matrices():
    poisson = 0.3
    lame_first = poisson / ((1.0 + poisson) * (1.0 - 2.0 * poisson))
    shear = 1.0 / (2.0 * (1.0 + poisson))
    elastic = np.zeros((6, 6))
    elastic[:3, :3] = lame_first
    for number in range(3):
        elastic[number, number] += 2.0 * shear
        elastic[number + 3, number + 3] = shear
    points = [0.5 - 0.5 / math.sqrt(3.0), 0.5 + 0.5 / math.sqrt(3.0)]
    corners = [(a, b, c) for a in (0, 1) for b in (0, 1) for c in (0, 1)]
    stiff = np.zeros((24, 24))
    for point_x in points:
        for point_y in points:
            for point_z in points:
                strain = np.zeros((6, 24))
                for number, corner in enumerate(corners):
                    shape_x = point_x if corner[0] else 1.0 - point_x
                    shape_y = point_y if corner[1] else 1.0 - point_y
                    shape_z = point_z if corner[2] else 1.0 - point_z
                    deriv_x = (2.0 * corner[0] - 1.0) * shape_y * shape_z
                    deriv_y = shape_x * (2.0 * corner[1] - 1.0) * shape_z
                    deriv_z = shape_x * shape_y * (2.0 * corner[2] - 1.0)
                    strain[0, 3 * number] = deriv_x
                    strain[1, 3 * number + 1] = deriv_y
                    strain[2, 3 * number + 2] = deriv_z
                    strain[3, 3 * number] = deriv_y
                    strain[3, 3 * number + 1] = deriv_x
                    strain[4, 3 * number + 1] = deriv_z
                    strain[4, 3 * number + 2] = deriv_y
                    strain[5, 3 * number] = deriv_z
                    strain[5, 3 * number + 2] = deriv_x
                stiff += strain.T @ elastic @ strain / 8.0
    line = np.array([[1.0 / 3.0, 1.0 / 6.0], [1.0 / 6.0, 1.0 / 3.0]])
    mass = np.kron(np.kron(line, line), line)
    return stiff, mass


def factors():
    stiff, mass = hex_matrices()
    pair = np.array([[1.0, 1.0], [-1.0, 1.0]])
    modes = np.kron(np.kron(pair, pair), pair)
    mass_weight = np.sqrt(np.diag(modes @ mass @ modes.T) / 64.0)
    both = np.kron(modes, np.eye(3))
    blocks = both @ stiff @ both.T / 64.0
    rows = []
    for label in range(8):
        index = [(label ^ (4 >> comp)) * 3 + comp for comp in range(3)]
        block = blocks[np.ix_(index, index)].copy()
        for k in range(3):
            if block[k, k] > 1e-9:
                row = block[k] / math.sqrt(block[k, k])
                rows.append([(index[b], float(row[b])) for b in range(3) if abs(row[b]) > 1e-9])
                block -= np.outer(row, row)
        assert np.abs(block).max() < 1e-9
    return mass_weight, rows


def pack_body(group, comps, planes, plane, chunks, x_ref, out_ref):
    stride = x_ref.shape[0] // group
    width_y = stride // (comps * planes)
    own = width_y // chunks
    for comp in range(comps):
        for y in range(width_y):
            start = (comp * planes + plane) * width_y + y
            value = x_ref[pl.ds(start, group, stride=stride), :]
            out_ref[y // own, comp * (own + 1) + y % own] = value
            if y % own == 0:
                out_ref[(y // own - 1) % chunks, comp * (own + 1) + own] = value


def pack_plane(basis, plane, chunks):
    group, comps, planes, width_y, width_z = basis.shape
    own = width_y // chunks
    return pl.pallas_call(
        functools.partial(pack_body, group, comps, planes, plane, chunks),
        out_shape=jax.ShapeDtypeStruct((chunks, comps * (own + 1), group, width_z), F32),
        in_specs=[pl.BlockSpec(memory_space=VMEM)],
        out_specs=pl.BlockSpec(memory_space=VMEM),
        name="pack",
    )(basis.reshape(-1, width_z))


def gram_body(scale, r0_ref, r1_ref, r2_ref, w_ref, out_ref, z_ref, mass_ref, stiff_ref):
    mass_weight, stiff_rows = factors()
    planes = (r0_ref, r1_ref, r2_ref)
    columns = 192
    n_mass = 24 * 128
    mass_ref[...] = jnp.zeros_like(mass_ref)
    stiff_ref[...] = jnp.zeros_like(stiff_ref)
    for i in range(2):
        for j in range(2):
            root = w_ref[0, i, pl.ds(j, 1), :]
            cubed = w_ref[1, i, pl.ds(j, 1), :]

            def step(q, carry):
                for g in range(3):
                    modes = {}
                    for comp in range(3):
                        lines = {}
                        for a in range(2):
                            for b in range(2):
                                parts = []
                                for n in (2 * g, 2 * g + 1):
                                    t = n % 3
                                    parts.append(
                                        planes[i + a][2 * q + n // 3, comp * 3 + j + b, 8 * t : 8 * t + 8, :]
                                    )
                                here = jnp.concatenate(parts, axis=0)
                                there = pltpu.roll(here, 127, 1)
                                lines[a, b, 0] = here + there
                                lines[a, b, 1] = there - here
                        faces = {}
                        for a in range(2):
                            for pc in range(2):
                                faces[a, 0, pc] = lines[a, 1, pc] + lines[a, 0, pc]
                                faces[a, 1, pc] = lines[a, 1, pc] - lines[a, 0, pc]
                        for pb in range(2):
                            for pc in range(2):
                                low, high = faces[0, pb, pc], faces[1, pb, pc]
                                modes[(2 * pb + pc) * 3 + comp] = high + low
                                modes[(4 + 2 * pb + pc) * 3 + comp] = high - low
                    start = pl.multiple_of(q * 48 + g * 16, 16)

                    def put(slot, value):
                        high = value.astype(BF16)
                        low = (value - high.astype(F32)).astype(BF16)
                        z_ref[pl.ds(start, 16), slot * 128 : slot * 128 + 128] = high
                        z_ref[pl.ds(columns + start, 16), slot * 128 : slot * 128 + 128] = low

                    for mode in range(24):
                        put(mode, modes[mode] * (root * float(mass_weight[mode // 3])))
                    for number, row in enumerate(stiff_rows):
                        total = None
                        for mode, coef in row:
                            term = modes[mode] * (cubed * coef)
                            total = term if total is None else total + term
                        put(24 + number, total)
                return carry

            lax.fori_loop(0, 4, step, 0)
            contract = (((1,), (1,)), ((), ()))
            mass_ref[...] += lax.dot_general(
                z_ref[:, :n_mass], z_ref[:columns, :n_mass], contract, preferred_element_type=F32
            )
            stiff_ref[...] += lax.dot_general(
                z_ref[:, n_mass:], z_ref[:columns, n_mass:], contract, preferred_element_type=F32
            )

    def whole(ref):
        cross = ref[columns:, :]
        return (ref[:columns, :] + cross + cross.T) * scale

    mass, stiff = whole(mass_ref), whole(stiff_ref)
    row = lax.broadcasted_iota(jnp.int32, (columns, columns), 0)
    col = lax.broadcasted_iota(jnp.int32, (columns, columns), 1)
    mixed = jnp.where(row >= col, stiff, mass)
    diagonal = jnp.sum(jnp.where(row == col, mass, 0.0), axis=1, keepdims=True)
    out_ref[:columns, :] = mixed[:, :128]
    out_ref[columns:, :64] = mixed[:, 128:]
    out_ref[columns:, 64:] = jnp.broadcast_to(diagonal, (columns, 64))


def gram(r0, r1, r2, weights, scale):
    slots = 24 + len(factors()[1])
    return pl.pallas_call(
        functools.partial(gram_body, scale),
        out_shape=jax.ShapeDtypeStruct((384, 128), F32),
        in_specs=[pl.BlockSpec(memory_space=VMEM)] * 4,
        out_specs=pl.BlockSpec(memory_space=VMEM),
        scratch_shapes=[
            VMEM((384, slots * 128), BF16),
            VMEM((384, 192), F32),
            VMEM((384, 192), F32),
        ],
        compiler_params=pltpu.CompilerParams(vmem_limit_bytes=48 * 2**20),
        name="gram",
    )(r0, r1, r2, weights)


def dot32(a, b, contract=((1,), (0,))):
    return lax.dot_general(
        a, b, (contract, ((), ())), precision=lax.Precision.HIGHEST, preferred_element_type=F32
    )


def eliminate(block):
    size = block.shape[0]
    row = lax.broadcasted_iota(jnp.int32, (size, size), 0)
    col = lax.broadcasted_iota(jnp.int32, (size, size), 1)
    unit = jnp.where(row == col, 1.0, 0.0).astype(F32)
    work = jnp.concatenate([block, unit], axis=1)
    pieces = [work[8 * t : 8 * t + 8, :] for t in range(size // 8)]
    sub = lax.broadcasted_iota(jnp.int32, (8, 128), 0)
    for j in range(size):
        at, inner = j // 8, j % 8
        line = pieces[at][inner : inner + 1, :]
        ratio = line / line[:, j : j + 1]
        for t in range(at, size // 8):
            factor = pieces[t][:, j : j + 1]
            change = factor * ratio
            if t == at:
                change = jnp.where(sub > inner, change, 0.0)
            pieces[t] = pieces[t] - change
    work = jnp.concatenate(pieces, axis=0)
    pivots = jnp.sum(jnp.where(row == col, work[:, :size], 0.0), axis=1, keepdims=True)
    root = lax.rsqrt(pivots)
    root = root * (1.5 - 0.5 * pivots * root * root)
    return work[:, size:] * root


def split(value):
    high = value.astype(BF16)
    return high, (value - high.astype(F32)).astype(BF16)


def solve_body(g_ref, r0_ref, r1_ref, send_ref, inverse_ref, stiff_ref, a_ref):
    columns, size = 192, 64
    packed = g_ref[...].reshape(384, 128)
    mixed = jnp.concatenate([packed[:columns], packed[columns:, :64]], axis=1)
    diagonal = packed[columns:, 64:65]
    row = lax.broadcasted_iota(jnp.int32, (columns, columns), 0)
    col = lax.broadcasted_iota(jnp.int32, (columns, columns), 1)
    other = mixed.T
    stiff_ref[...] = jnp.where(row >= col, mixed, other)
    mass = jnp.where(row < col, mixed, jnp.where(row == col, diagonal, other))
    a_ref[...] = jnp.zeros_like(a_ref)
    a_ref[:, :columns] = mass
    a_ref[:, 256 : 256 + columns] = jnp.where(row == col, 1.0, 0.0).astype(F32)
    for k in range(columns // size):
        low, high = k * size, k * size + size
        lines = dot32(eliminate(a_ref[low:high, low:high]), a_ref[low:high, :])
        a_ref[low:high, :] = lines
        if high < columns:
            a_ref[high:, :] -= dot32(lines[:, high:columns], lines, ((0,), (0,)))
    inverse = a_ref[:, 256 : 256 + columns]
    inverse_ref[...] = inverse
    left_high, left_low = split(inverse)
    for plane, ref in enumerate((r0_ref, r1_ref)):
        for comp in range(3):
            pair = [ref[:, comp * 3 + j].reshape(columns, 128) for j in range(2)]
            right_high, right_low = split(jnp.concatenate(pair, axis=1))
            total = jnp.dot(left_high, right_high, preferred_element_type=F32)
            total += jnp.dot(left_high, right_low, preferred_element_type=F32)
            total += jnp.dot(left_low, right_high, preferred_element_type=F32)
            for j in range(2):
                slot = (comp * 2 + plane) * 2 + j
                send_ref[:, slot] = total[:, 128 * j : 128 * j + 128].reshape(8, 24, 128)


def solve(packed, r0, r1):
    return pl.pallas_call(
        solve_body,
        out_shape=(
            jax.ShapeDtypeStruct((8, 12, 24, 128), F32),
            jax.ShapeDtypeStruct((192, 192), F32),
            jax.ShapeDtypeStruct((192, 192), F32),
        ),
        in_specs=[pl.BlockSpec(memory_space=VMEM)] * 3,
        out_specs=[pl.BlockSpec(memory_space=VMEM)] * 3,
        scratch_shapes=[VMEM((192, 512), F32)],
        compiler_params=pltpu.CompilerParams(vmem_limit_bytes=48 * 2**20),
        name="solve",
    )(packed, r0, r1)


def unpack_body(t_ref, out_ref):
    for source in range(8):
        for comp in range(3):
            for plane in range(2):
                for j in range(2):
                    start = (comp * 2 + plane) * 16 + 2 * source + j
                    slot = (comp * 2 + plane) * 2 + j
                    out_ref[pl.ds(start, 24, stride=96), :] = t_ref[source, slot]


def unpack(received):
    return pl.pallas_call(
        unpack_body,
        out_shape=jax.ShapeDtypeStruct((2304, 128), F32),
        in_specs=[pl.BlockSpec(memory_space=VMEM)],
        out_specs=pl.BlockSpec(memory_space=VMEM),
        name="unpack",
    )(received)


def exchange(value, axes):
    return lax.all_to_all(value, axes, 0, 0)


def copies(value, count):
    return jnp.broadcast_to(value[None], (count,) + value.shape)


def per_device(basis, density):
    chunks = lax.axis_size(MODE)
    slabs = lax.axis_size(SPACE)
    width_y = basis.shape[3]
    own = width_y // chunks
    scale = 1.0 / (3.0 * basis.shape[2] * width_y * basis.shape[4] * slabs)
    density = lax.dynamic_slice_in_dim(density, lax.axis_index(MODE) * own, own, axis=1)
    root = jnp.sqrt(density)
    weights = jnp.stack([root, density * root])

    r0 = exchange(pack_plane(basis, 0, chunks), MODE)
    second, r0 = lax.optimization_barrier((pack_plane(basis, 1, chunks), r0))
    r2 = lax.ppermute(r0, SPACE, [(i, i - 1) for i in range(1, slabs)])
    r1 = exchange(second, MODE)
    part = gram(r0, r1, r2, weights, scale)

    plane_axes, line_axes = MODE + ("yh",), ("zc",)
    first, last = lax.axis_size(plane_axes), lax.axis_size(line_axes)
    piece = exchange(part.reshape(first, 384 // first, 128), plane_axes).sum(0)
    piece = exchange(copies(piece, last), line_axes).sum(0)
    packed = exchange(copies(piece, first), plane_axes)

    send, inverse, stiff = solve(packed, r0, r1)
    rotated = unpack(exchange(send, MODE)).reshape(basis.shape)
    high = lax.Precision.HIGHEST
    reduced = jnp.dot(jnp.dot(inverse, stiff, precision=high), inverse.T, precision=high)
    return rotated, reduced


def solution(mesh):
    modes, slabs = mesh.devices.shape
    half = 2 if slabs % 4 == 0 else 1
    inner = Mesh(mesh.devices.reshape(modes // 2, 2, half, slabs // half), MODE + SPACE)
    field = P(MODE, None, SPACE, None, None)
    return jax.shard_map(
        per_device,
        mesh=inner,
        in_specs=(field, P(SPACE, None, None)),
        out_specs=(field, P()),
        check_vma=False,
    )
```

```python
import functools
import math

import jax
import jax.numpy as jnp
import numpy as np
from jax import lax
from jax.experimental import pallas as pl
from jax.experimental.pallas import tpu as pltpu
from jax.sharding import Mesh, PartitionSpec as P

VMEM = pltpu.VMEM
MODE = ("x", "yl")
SPACE = ("yh", "zc")
F32 = jnp.float32
BF16 = jnp.bfloat16


def hex_matrices():
    poisson = 0.3
    lame_first = poisson / ((1.0 + poisson) * (1.0 - 2.0 * poisson))
    shear = 1.0 / (2.0 * (1.0 + poisson))
    elastic = np.zeros((6, 6))
    elastic[:3, :3] = lame_first
    for number in range(3):
        elastic[number, number] += 2.0 * shear
        elastic[number + 3, number + 3] = shear
    points = [0.5 - 0.5 / math.sqrt(3.0), 0.5 + 0.5 / math.sqrt(3.0)]
    corners = [(a, b, c) for a in (0, 1) for b in (0, 1) for c in (0, 1)]
    stiff = np.zeros((24, 24))
    for point_x in points:
        for point_y in points:
            for point_z in points:
                strain = np.zeros((6, 24))
                for number, corner in enumerate(corners):
                    shape_x = point_x if corner[0] else 1.0 - point_x
                    shape_y = point_y if corner[1] else 1.0 - point_y
                    shape_z = point_z if corner[2] else 1.0 - point_z
                    deriv_x = (2.0 * corner[0] - 1.0) * shape_y * shape_z
                    deriv_y = shape_x * (2.0 * corner[1] - 1.0) * shape_z
                    deriv_z = shape_x * shape_y * (2.0 * corner[2] - 1.0)
                    strain[0, 3 * number] = deriv_x
                    strain[1, 3 * number + 1] = deriv_y
                    strain[2, 3 * number + 2] = deriv_z
                    strain[3, 3 * number] = deriv_y
                    strain[3, 3 * number + 1] = deriv_x
                    strain[4, 3 * number + 1] = deriv_z
                    strain[4, 3 * number + 2] = deriv_y
                    strain[5, 3 * number] = deriv_z
                    strain[5, 3 * number + 2] = deriv_x
                stiff += strain.T @ elastic @ strain / 8.0
    line = np.array([[1.0 / 3.0, 1.0 / 6.0], [1.0 / 6.0, 1.0 / 3.0]])
    mass = np.kron(np.kron(line, line), line)
    return stiff, mass


def factors():
    stiff, mass = hex_matrices()
    pair = np.array([[1.0, 1.0], [-1.0, 1.0]])
    modes = np.kron(np.kron(pair, pair), pair)
    mass_weight = np.sqrt(np.diag(modes @ mass @ modes.T) / 64.0)
    both = np.kron(modes, np.eye(3))
    blocks = both @ stiff @ both.T / 64.0
    rows = []
    for label in range(8):
        index = [(label ^ (4 >> comp)) * 3 + comp for comp in range(3)]
        block = blocks[np.ix_(index, index)].copy()
        for k in range(3):
            if block[k, k] > 1e-9:
                row = block[k] / math.sqrt(block[k, k])
                rows.append([(index[b], float(row[b])) for b in range(3) if abs(row[b]) > 1e-9])
                block -= np.outer(row, row)
        assert np.abs(block).max() < 1e-9
    return mass_weight, rows


def pack_body(group, comps, planes, plane, chunks, x_ref, out_ref):
    stride = x_ref.shape[0] // group
    width_y = stride // (comps * planes)
    own = width_y // chunks
    for comp in range(comps):
        for y in range(width_y):
            start = (comp * planes + plane) * width_y + y
            value = x_ref[pl.ds(start, group, stride=stride), :]
            out_ref[y // own, comp * (own + 1) + y % own] = value
            if y % own == 0:
                out_ref[(y // own - 1) % chunks, comp * (own + 1) + own] = value


def pack_plane(basis, plane, chunks):
    group, comps, planes, width_y, width_z = basis.shape
    own = width_y // chunks
    return pl.pallas_call(
        functools.partial(pack_body, group, comps, planes, plane, chunks),
        out_shape=jax.ShapeDtypeStruct((chunks, comps * (own + 1), group, width_z), F32),
        in_specs=[pl.BlockSpec(memory_space=VMEM)],
        out_specs=pl.BlockSpec(memory_space=VMEM),
        name="pack",
    )(basis.reshape(-1, width_z))


def gram_body(scale, r0_ref, r1_ref, r2_ref, w_ref, out_ref, z_ref, mass_ref, stiff_ref):
    mass_weight, stiff_rows = factors()
    planes = (r0_ref, r1_ref, r2_ref)
    columns = 192
    n_mass = 24 * 128
    mass_ref[...] = jnp.zeros_like(mass_ref)
    stiff_ref[...] = jnp.zeros_like(stiff_ref)
    for i in range(2):
        for j in range(2):
            root = w_ref[0, i, pl.ds(j, 1), :]
            cubed = w_ref[1, i, pl.ds(j, 1), :]

            def step(q, carry):
                for g in range(3):
                    modes = {}
                    for comp in range(3):
                        lines = {}
                        for a in range(2):
                            for b in range(2):
                                parts = []
                                for n in (2 * g, 2 * g + 1):
                                    t = n % 3
                                    parts.append(
                                        planes[i + a][2 * q + n // 3, comp * 3 + j + b, 8 * t : 8 * t + 8, :]
                                    )
                                here = jnp.concatenate(parts, axis=0)
                                there = pltpu.roll(here, 127, 1)
                                lines[a, b, 0] = here + there
                                lines[a, b, 1] = there - here
                        faces = {}
                        for a in range(2):
                            for pc in range(2):
                                faces[a, 0, pc] = lines[a, 1, pc] + lines[a, 0, pc]
                                faces[a, 1, pc] = lines[a, 1, pc] - lines[a, 0, pc]
                        for pb in range(2):
                            for pc in range(2):
                                low, high = faces[0, pb, pc], faces[1, pb, pc]
                                modes[(2 * pb + pc) * 3 + comp] = high + low
                                modes[(4 + 2 * pb + pc) * 3 + comp] = high - low
                    start = pl.multiple_of(q * 48 + g * 16, 16)

                    def put(slot, value):
                        high = value.astype(BF16)
                        low = (value - high.astype(F32)).astype(BF16)
                        z_ref[pl.ds(start, 16), slot * 128 : slot * 128 + 128] = high
                        z_ref[pl.ds(columns + start, 16), slot * 128 : slot * 128 + 128] = low

                    for mode in range(24):
                        put(mode, modes[mode] * (root * float(mass_weight[mode // 3])))
                    for number, row in enumerate(stiff_rows):
                        total = None
                        for mode, coef in row:
                            term = modes[mode] * (cubed * coef)
                            total = term if total is None else total + term
                        put(24 + number, total)
                return carry

            lax.fori_loop(0, 4, step, 0)
            contract = (((1,), (1,)), ((), ()))
            mass_ref[...] += lax.dot_general(
                z_ref[:, :n_mass], z_ref[:columns, :n_mass], contract, preferred_element_type=F32
            )
            stiff_ref[...] += lax.dot_general(
                z_ref[:, n_mass:], z_ref[:columns, n_mass:], contract, preferred_element_type=F32
            )

    def whole(ref):
        cross = ref[columns:, :]
        return (ref[:columns, :] + cross + cross.T) * scale

    mass, stiff = whole(mass_ref), whole(stiff_ref)
    row = lax.broadcasted_iota(jnp.int32, (columns, columns), 0)
    col = lax.broadcasted_iota(jnp.int32, (columns, columns), 1)
    mixed = jnp.where(row >= col, stiff, mass)
    diagonal = jnp.sum(jnp.where(row == col, mass, 0.0), axis=1, keepdims=True)
    out_ref[:columns, :] = mixed[:, :128]
    out_ref[columns:, :64] = mixed[:, 128:]
    out_ref[columns:, 64:] = jnp.broadcast_to(diagonal, (columns, 64))


def gram(r0, r1, r2, weights, scale):
    slots = 24 + len(factors()[1])
    return pl.pallas_call(
        functools.partial(gram_body, scale),
        out_shape=jax.ShapeDtypeStruct((384, 128), F32),
        in_specs=[pl.BlockSpec(memory_space=VMEM)] * 4,
        out_specs=pl.BlockSpec(memory_space=VMEM),
        scratch_shapes=[
            VMEM((384, slots * 128), BF16),
            VMEM((384, 192), F32),
            VMEM((384, 192), F32),
        ],
        compiler_params=pltpu.CompilerParams(vmem_limit_bytes=48 * 2**20),
        name="gram",
    )(r0, r1, r2, weights)


def dot32(a, b, contract=((1,), (0,))):
    return lax.dot_general(
        a, b, (contract, ((), ())), precision=lax.Precision.HIGHEST, preferred_element_type=F32
    )


def eliminate(block):
    size = block.shape[0]
    groups = size // 8
    sub = lax.broadcasted_iota(jnp.int32, (8, 128), 0)
    lane = lax.broadcasted_iota(jnp.int32, (8, 128), 1)
    spread = {}
    for k in range(size):
        for t in range(k // 8, groups):
            spread[k, t] = jnp.broadcast_to(block[8 * t : 8 * t + 8, k : k + 1], (8, 128))
    right = [jnp.where(lane == sub + 8 * t, 1.0, 0.0).astype(F32) for t in range(groups)]
    for i in range(size):
        at, inner = i // 8, i % 8
        inverse = 1.0 / spread[i, at][inner : inner + 1, :]
        factor = {t: spread[i, t] * inverse for t in range(at, groups)}
        factor[at] = jnp.where(sub > inner, factor[at], 0.0)
        for k in range(i + 1, size):
            entry = spread[i, k // 8][k % 8 : k % 8 + 1, :]
            for t in range(k // 8, groups):
                spread[k, t] = spread[k, t] - factor[t] * entry
        line = right[at][inner : inner + 1, :]
        for t in range(at, groups):
            right[t] = right[t] - factor[t] * line
    for t in range(groups):
        pivots = spread[8 * t, t]
        for inner in range(1, 8):
            pivots = jnp.where(sub == inner, spread[8 * t + inner, t], pivots)
        root = lax.rsqrt(pivots)
        right[t] = right[t] * (root * (1.5 - 0.5 * pivots * root * root))
    return jnp.concatenate(right, axis=0)[:, :size]


def split(value):
    high = value.astype(BF16)
    return high, (value - high.astype(F32)).astype(BF16)


def solve_body(g_ref, r0_ref, r1_ref, send_ref, inverse_ref, stiff_ref, a_ref):
    columns, size = 192, 32
    packed = g_ref[...].reshape(384, 128)
    mixed = jnp.concatenate([packed[:columns], packed[columns:, :64]], axis=1)
    diagonal = packed[columns:, 64:65]
    row = lax.broadcasted_iota(jnp.int32, (columns, columns), 0)
    col = lax.broadcasted_iota(jnp.int32, (columns, columns), 1)
    other = mixed.T
    stiff_ref[...] = jnp.where(row >= col, mixed, other)
    mass = jnp.where(row < col, mixed, jnp.where(row == col, diagonal, other))
    a_ref[...] = jnp.zeros_like(a_ref)
    a_ref[:, :columns] = mass
    a_ref[:, 256 : 256 + columns] = jnp.where(row == col, 1.0, 0.0).astype(F32)
    for k in range(columns // size):
        low, high = k * size, k * size + size
        lines = dot32(eliminate(a_ref[low:high, low:high]), a_ref[low:high, :])
        a_ref[low:high, :] = lines
        if high < columns:
            a_ref[high:, :] -= dot32(lines[:, high:columns], lines, ((0,), (0,)))
    inverse = a_ref[:, 256 : 256 + columns]
    inverse_ref[...] = inverse
    left_high, left_low = split(inverse)
    for plane, ref in enumerate((r0_ref, r1_ref)):
        for comp in range(3):
            pair = [ref[:, comp * 3 + j].reshape(columns, 128) for j in range(2)]
            right_high, right_low = split(jnp.concatenate(pair, axis=1))
            total = jnp.dot(left_high, right_high, preferred_element_type=F32)
            total += jnp.dot(left_high, right_low, preferred_element_type=F32)
            total += jnp.dot(left_low, right_high, preferred_element_type=F32)
            for j in range(2):
                slot = (comp * 2 + plane) * 2 + j
                send_ref[:, slot] = total[:, 128 * j : 128 * j + 128].reshape(8, 24, 128)


def solve(packed, r0, r1):
    return pl.pallas_call(
        solve_body,
        out_shape=(
            jax.ShapeDtypeStruct((8, 12, 24, 128), F32),
            jax.ShapeDtypeStruct((192, 192), F32),
            jax.ShapeDtypeStruct((192, 192), F32),
        ),
        in_specs=[pl.BlockSpec(memory_space=VMEM)] * 3,
        out_specs=[pl.BlockSpec(memory_space=VMEM)] * 3,
        scratch_shapes=[VMEM((192, 512), F32)],
        compiler_params=pltpu.CompilerParams(vmem_limit_bytes=48 * 2**20),
        name="solve",
    )(packed, r0, r1)


def unpack_body(t_ref, out_ref):
    for source in range(8):
        for comp in range(3):
            for plane in range(2):
                for j in range(2):
                    start = (comp * 2 + plane) * 16 + 2 * source + j
                    slot = (comp * 2 + plane) * 2 + j
                    out_ref[pl.ds(start, 24, stride=96), :] = t_ref[source, slot]


def unpack(received):
    return pl.pallas_call(
        unpack_body,
        out_shape=jax.ShapeDtypeStruct((2304, 128), F32),
        in_specs=[pl.BlockSpec(memory_space=VMEM)],
        out_specs=pl.BlockSpec(memory_space=VMEM),
        name="unpack",
    )(received)


def exchange(value, axes):
    return lax.all_to_all(value, axes, 0, 0)


def copies(value, count):
    return jnp.broadcast_to(value[None], (count,) + value.shape)


def per_device(basis, density):
    chunks = lax.axis_size(MODE)
    slabs = lax.axis_size(SPACE)
    width_y = basis.shape[3]
    own = width_y // chunks
    scale = 1.0 / (3.0 * basis.shape[2] * width_y * basis.shape[4] * slabs)
    density = lax.dynamic_slice_in_dim(density, lax.axis_index(MODE) * own, own, axis=1)
    root = jnp.sqrt(density)
    weights = jnp.stack([root, density * root])

    r0 = exchange(pack_plane(basis, 0, chunks), MODE)
    second, r0 = lax.optimization_barrier((pack_plane(basis, 1, chunks), r0))
    r2 = lax.ppermute(r0, SPACE, [(i, i - 1) for i in range(1, slabs)])
    r1 = exchange(second, MODE)
    part = gram(r0, r1, r2, weights, scale)

    plane_axes, line_axes = MODE + ("yh",), ("zc",)
    first, last = lax.axis_size(plane_axes), lax.axis_size(line_axes)
    piece = exchange(part.reshape(first, 384 // first, 128), plane_axes).sum(0)
    piece = exchange(copies(piece, last), line_axes).sum(0)
    packed = exchange(copies(piece, first), plane_axes)

    send, inverse, stiff = solve(packed, r0, r1)
    rotated = unpack(exchange(send, MODE)).reshape(basis.shape)
    high = lax.Precision.HIGHEST
    reduced = jnp.dot(jnp.dot(inverse, stiff, precision=high), inverse.T, precision=high)
    return rotated, reduced


def solution(mesh):
    modes, slabs = mesh.devices.shape
    half = 2 if slabs % 4 == 0 else 1
    inner = Mesh(mesh.devices.reshape(modes // 2, 2, half, slabs // half), MODE + SPACE)
    field = P(MODE, None, SPACE, None, None)
    return jax.shard_map(
        per_device,
        mesh=inner,
        in_specs=(field, P(SPACE, None, None)),
        out_specs=(field, P()),
        check_vma=False,
    )
```

```python
import functools
import math

import jax
import jax.numpy as jnp
import numpy as np
from jax import lax
from jax.experimental import pallas as pl
from jax.experimental.pallas import tpu as pltpu
from jax.sharding import Mesh, PartitionSpec as P

VMEM = pltpu.VMEM
MODE = ("x", "yl")
SPACE = ("yh", "zc")
F32 = jnp.float32
BF16 = jnp.bfloat16


def hex_matrices():
    poisson = 0.3
    lame_first = poisson / ((1.0 + poisson) * (1.0 - 2.0 * poisson))
    shear = 1.0 / (2.0 * (1.0 + poisson))
    elastic = np.zeros((6, 6))
    elastic[:3, :3] = lame_first
    for number in range(3):
        elastic[number, number] += 2.0 * shear
        elastic[number + 3, number + 3] = shear
    points = [0.5 - 0.5 / math.sqrt(3.0), 0.5 + 0.5 / math.sqrt(3.0)]
    corners = [(a, b, c) for a in (0, 1) for b in (0, 1) for c in (0, 1)]
    stiff = np.zeros((24, 24))
    for point_x in points:
        for point_y in points:
            for point_z in points:
                strain = np.zeros((6, 24))
                for number, corner in enumerate(corners):
                    shape_x = point_x if corner[0] else 1.0 - point_x
                    shape_y = point_y if corner[1] else 1.0 - point_y
                    shape_z = point_z if corner[2] else 1.0 - point_z
                    deriv_x = (2.0 * corner[0] - 1.0) * shape_y * shape_z
                    deriv_y = shape_x * (2.0 * corner[1] - 1.0) * shape_z
                    deriv_z = shape_x * shape_y * (2.0 * corner[2] - 1.0)
                    strain[0, 3 * number] = deriv_x
                    strain[1, 3 * number + 1] = deriv_y
                    strain[2, 3 * number + 2] = deriv_z
                    strain[3, 3 * number] = deriv_y
                    strain[3, 3 * number + 1] = deriv_x
                    strain[4, 3 * number + 1] = deriv_z
                    strain[4, 3 * number + 2] = deriv_y
                    strain[5, 3 * number] = deriv_z
                    strain[5, 3 * number + 2] = deriv_x
                stiff += strain.T @ elastic @ strain / 8.0
    line = np.array([[1.0 / 3.0, 1.0 / 6.0], [1.0 / 6.0, 1.0 / 3.0]])
    mass = np.kron(np.kron(line, line), line)
    return stiff, mass


def factors():
    stiff, mass = hex_matrices()
    pair = np.array([[1.0, 1.0], [-1.0, 1.0]])
    modes = np.kron(np.kron(pair, pair), pair)
    mass_weight = np.sqrt(np.diag(modes @ mass @ modes.T) / 64.0)
    both = np.kron(modes, np.eye(3))
    blocks = both @ stiff @ both.T / 64.0
    rows = []
    for label in range(8):
        index = [(label ^ (4 >> comp)) * 3 + comp for comp in range(3)]
        block = blocks[np.ix_(index, index)].copy()
        for k in range(3):
            if block[k, k] > 1e-9:
                row = block[k] / math.sqrt(block[k, k])
                rows.append([(index[b], float(row[b])) for b in range(3) if abs(row[b]) > 1e-9])
                block -= np.outer(row, row)
        assert np.abs(block).max() < 1e-9
    return mass_weight, rows


def swap_blocks(vectors):
    block = lax.broadcasted_iota(jnp.int32, vectors[0].shape, 1) // 16
    vectors = [pltpu.roll(v, 16 * k, 1) if k else v for k, v in enumerate(vectors)]
    for step in (1, 2, 4):
        moved = (block & step) != 0
        vectors = [jnp.where(moved, vectors[(k + step) % 8], vectors[k]) for k in range(8)]
    return [pltpu.roll(vectors[-k % 8], 128 - 16 * k, 1) if k else vectors[0] for k in range(8)]


def slot_of(plane, comp, half):
    return (1 - plane) * 6 + comp * 2 + half


def edge_lane(plane, comp, half):
    return half * 6 + plane * 3 + comp


def pack_body(x_ref, out_ref):
    for plane in range(2):
        for comp in range(3):
            first = (comp * 2 + plane) * 16
            lines = jnp.swapaxes(x_ref[:, first : first + 16, :], 0, 1)
            for half in range(2):
                parts = swap_blocks([lines[2 * k + half] for k in range(8)])
                for chunk in range(8):
                    out_ref[chunk, slot_of(plane, comp, half)] = parts[chunk]
    within = lax.broadcasted_iota(jnp.int32, (24, 128), 1) % 16
    for chunk in range(8):
        edge = jnp.zeros((24, 128), F32)
        for plane in range(2):
            for comp in range(3):
                for half in range(2):
                    lane = edge_lane(plane, comp, half)
                    value = out_ref[(chunk + 1) % 8, slot_of(plane, comp, half)]
                    edge = jnp.where(within == lane, pltpu.roll(value, lane, 1), edge)
        out_ref[chunk, 12] = edge


def pack(basis):
    return pl.pallas_call(
        pack_body,
        out_shape=jax.ShapeDtypeStruct((8, 13, 24, 128), F32),
        in_specs=[pl.BlockSpec(memory_space=VMEM)],
        out_specs=pl.BlockSpec(memory_space=VMEM),
        name="pack",
    )(basis.reshape(24, 96, 128))


def gram_body(scale, layer, near_ref, far_ref, w_ref, *rest):
    if layer == 0:
        before_ref, (out_ref, mass_ref, stiff_ref) = None, rest
        places = ((near_ref, 0, 0), (near_ref, 1, 0))
    else:
        before_ref, out_ref, mass_ref, stiff_ref = rest
        places = ((near_ref, 1, 0), (far_ref, 0, 6))
    mass_weight, stiff_rows = factors()
    columns = 192
    last = lax.broadcasted_iota(jnp.int32, (16, 128), 1) % 16 == 15

    def read(ref, q, g, slot):
        parts = []
        for n in (2 * g, 2 * g + 1):
            t = n % 3
            parts.append(ref[2 * q + n // 3, slot, 8 * t : 8 * t + 8, :])
        return jnp.concatenate(parts, axis=0)

    def step(q, carry):
        for g in range(3):
            modes = {}
            edges = [read(ref, q, g, 12 - back) for ref, _, back in places]
            for comp in range(3):
                faces = {}
                for a, (ref, plane, back) in enumerate(places):
                    lines = {}
                    for half in range(2):
                        here = read(ref, q, g, slot_of(plane, comp, half) - back)
                        edge = pltpu.roll(edges[a], 15 - edge_lane(plane, comp, half), 1)
                        there = jnp.where(last, edge, pltpu.roll(here, 127, 1))
                        lines[half, 0] = here + there
                        lines[half, 1] = there - here
                    for pc in range(2):
                        even, odd = lines[0, pc], lines[1, pc]
                        following = pltpu.roll(even, 112, 1)
                        faces[a, 0, 0, pc] = odd + even
                        faces[a, 0, 1, pc] = odd - even
                        faces[a, 1, 0, pc] = following + odd
                        faces[a, 1, 1, pc] = following - odd
                for half in range(2):
                    for pb in range(2):
                        for pc in range(2):
                            low, high = faces[0, half, pb, pc], faces[1, half, pb, pc]
                            modes[half, (2 * pb + pc) * 3 + comp] = high + low
                            modes[half, (4 + 2 * pb + pc) * 3 + comp] = high - low
            start = pl.multiple_of(q * 48 + g * 16, 16)

            def put(ref, slot, value):
                high = value.astype(BF16)
                low = (value - high.astype(F32)).astype(BF16)
                ref[pl.ds(start, 16), slot * 128 : slot * 128 + 128] = high
                ref[pl.ds(columns + start, 16), slot * 128 : slot * 128 + 128] = low

            for half in range(2):
                root = w_ref[0, layer, pl.ds(half, 1), :]
                cubed = w_ref[1, layer, pl.ds(half, 1), :]
                for mode in range(24):
                    value = modes[half, mode] * (root * float(mass_weight[mode // 3]))
                    put(mass_ref, 24 * half + mode, value)
                for number, row in enumerate(stiff_rows):
                    total = None
                    for mode, coef in row:
                        term = modes[half, mode] * (cubed * coef)
                        total = term if total is None else total + term
                    put(stiff_ref, len(stiff_rows) * half + number, total)
        return carry

    lax.fori_loop(0, 4, step, 0)

    def whole(ref):
        both = lax.dot_general(
            ref[...], ref[:columns, :], (((1,), (1,)), ((), ())), preferred_element_type=F32
        )
        cross = both[columns:, :]
        return (both[:columns, :] + cross + cross.T) * scale

    mass, stiff = whole(mass_ref), whole(stiff_ref)
    row = lax.broadcasted_iota(jnp.int32, (columns, columns), 0)
    col = lax.broadcasted_iota(jnp.int32, (columns, columns), 1)
    mixed = jnp.where(row >= col, stiff, mass)
    diagonal = jnp.sum(jnp.where(row == col, mass, 0.0), axis=1, keepdims=True)
    out_ref[:columns, :] = mixed[:, :128]
    out_ref[columns:, :64] = mixed[:, 128:]
    out_ref[columns:, 64:] = jnp.broadcast_to(diagonal, (columns, 64))
    if before_ref is not None:
        out_ref[...] += before_ref[...]


def gram(layer, near, far, weights, scale, before=()):
    stiff = len(factors()[1])
    return pl.pallas_call(
        functools.partial(gram_body, scale, layer),
        out_shape=jax.ShapeDtypeStruct((384, 128), F32),
        in_specs=[pl.BlockSpec(memory_space=VMEM)] * (3 + len(before)),
        out_specs=pl.BlockSpec(memory_space=VMEM),
        scratch_shapes=[
            VMEM((384, 2 * 24 * 128), BF16),
            VMEM((384, 2 * stiff * 128), BF16),
        ],
        compiler_params=pltpu.CompilerParams(vmem_limit_bytes=48 * 2**20),
        cost_estimate=pl.CostEstimate(flops=3 * 10**9, bytes_accessed=3 * 10**6, transcendentals=0),
        name="gram",
    )(near, far, weights, *before)


def dot32(a, b, contract=((1,), (0,))):
    return lax.dot_general(
        a, b, (contract, ((), ())), precision=lax.Precision.HIGHEST, preferred_element_type=F32
    )


def eliminate(block):
    size = block.shape[0]
    groups = size // 8
    sub = lax.broadcasted_iota(jnp.int32, (8, 128), 0)
    lane = lax.broadcasted_iota(jnp.int32, (8, 128), 1)
    spread = {}
    for k in range(size):
        for t in range(k // 8, groups):
            spread[k, t] = jnp.broadcast_to(block[8 * t : 8 * t + 8, k : k + 1], (8, 128))
    right = [jnp.where(lane == sub + 8 * t, 1.0, 0.0).astype(F32) for t in range(groups)]
    for i in range(size):
        at, inner = i // 8, i % 8
        inverse = 1.0 / spread[i, at][inner : inner + 1, :]
        factor = {t: spread[i, t] * inverse for t in range(at, groups)}
        factor[at] = jnp.where(sub > inner, factor[at], 0.0)
        for k in range(i + 1, size):
            entry = spread[i, k // 8][k % 8 : k % 8 + 1, :]
            for t in range(k // 8, groups):
                spread[k, t] = spread[k, t] - factor[t] * entry
        line = right[at][inner : inner + 1, :]
        for t in range(at, groups):
            right[t] = right[t] - factor[t] * line
    for t in range(groups):
        pivots = spread[8 * t, t]
        for inner in range(1, 8):
            pivots = jnp.where(sub == inner, spread[8 * t + inner, t], pivots)
        root = lax.rsqrt(pivots)
        right[t] = right[t] * (root * (1.5 - 0.5 * pivots * root * root))
    return jnp.concatenate(right, axis=0)[:, :size]


def split(value):
    high = value.astype(BF16)
    return high, (value - high.astype(F32)).astype(BF16)


def solve_body(g_ref, r_ref, send_ref, inverse_ref, stiff_ref, a_ref):
    columns, size = 192, 32
    packed = g_ref[...].reshape(384, 128)
    mixed = jnp.concatenate([packed[:columns], packed[columns:, :64]], axis=1)
    diagonal = packed[columns:, 64:65]
    row = lax.broadcasted_iota(jnp.int32, (columns, columns), 0)
    col = lax.broadcasted_iota(jnp.int32, (columns, columns), 1)
    other = mixed.T
    stiff_ref[...] = jnp.where(row >= col, mixed, other)
    mass = jnp.where(row < col, mixed, jnp.where(row == col, diagonal, other))
    a_ref[...] = jnp.zeros_like(a_ref)
    a_ref[:, :columns] = mass
    a_ref[:, 256 : 256 + columns] = jnp.where(row == col, 1.0, 0.0).astype(F32)
    for k in range(columns // size):
        low, high = k * size, k * size + size
        lines = dot32(eliminate(a_ref[low:high, low:high]), a_ref[low:high, :])
        a_ref[low:high, :] = lines
        if high < columns:
            a_ref[high:, :] -= dot32(lines[:, high:columns], lines, ((0,), (0,)))
    inverse = a_ref[:, 256 : 256 + columns]
    inverse_ref[...] = inverse
    left_high, left_low = split(inverse)
    for pair in range(6):
        sides = [r_ref[:, 2 * pair + half].reshape(columns, 128) for half in range(2)]
        right_high, right_low = split(jnp.concatenate(sides, axis=1))
        total = jnp.dot(left_high, right_high, preferred_element_type=F32)
        total += jnp.dot(left_high, right_low, preferred_element_type=F32)
        total += jnp.dot(left_low, right_high, preferred_element_type=F32)
        for half in range(2):
            send_ref[:, 2 * pair + half] = total[:, 128 * half : 128 * half + 128].reshape(8, 24, 128)


def solve(packed, received):
    return pl.pallas_call(
        solve_body,
        out_shape=(
            jax.ShapeDtypeStruct((8, 12, 24, 128), F32),
            jax.ShapeDtypeStruct((192, 192), F32),
            jax.ShapeDtypeStruct((192, 192), F32),
        ),
        in_specs=[pl.BlockSpec(memory_space=VMEM)] * 2,
        out_specs=[pl.BlockSpec(memory_space=VMEM)] * 3,
        scratch_shapes=[VMEM((192, 512), F32)],
        compiler_params=pltpu.CompilerParams(vmem_limit_bytes=48 * 2**20),
        name="solve",
    )(packed, received)


def unpack_body(t_ref, out_ref):
    for plane in range(2):
        for comp in range(3):
            lines = [None] * 16
            for half in range(2):
                slot = slot_of(plane, comp, half)
                lines[half::2] = swap_blocks([t_ref[chunk, slot] for chunk in range(8)])
            first = (comp * 2 + plane) * 16
            out_ref[:, first : first + 16, :] = jnp.swapaxes(jnp.stack(lines), 0, 1)


def unpack(received):
    return pl.pallas_call(
        unpack_body,
        out_shape=jax.ShapeDtypeStruct((24, 96, 128), F32),
        in_specs=[pl.BlockSpec(memory_space=VMEM)],
        out_specs=pl.BlockSpec(memory_space=VMEM),
        name="unpack",
    )(received)


def exchange(value, axes):
    return lax.all_to_all(value, axes, 0, 0)


def copies(value, count):
    return jnp.broadcast_to(value[None], (count,) + value.shape)


def per_device(basis, density):
    chunks = lax.axis_size(MODE)
    slabs = lax.axis_size(SPACE)
    planes, width_y, width_z = basis.shape[2:]
    own = width_z // chunks
    scale = 1.0 / (3.0 * planes * width_y * width_z * slabs)
    density = lax.dynamic_slice_in_dim(density, lax.axis_index(MODE) * own, own, axis=2)
    density = jnp.swapaxes(density.reshape(planes, width_y // 2, 2, own), 1, 2)
    density = density.reshape(planes, 2, width_y // 2 * own)
    root = jnp.sqrt(density)
    weights = jnp.stack([root, density * root])

    near = exchange(pack(basis), MODE)
    far = lax.ppermute(near[:, 6:], SPACE, [(i, i - 1) for i in range(1, slabs)])
    part = gram(0, near, near, weights, scale)
    part = gram(1, near, far, weights, scale, (part,))

    plane_axes, line_axes = MODE + ("yh",), ("zc",)
    first, last = lax.axis_size(plane_axes), lax.axis_size(line_axes)
    piece = exchange(part.reshape(first, 384 // first, 128), plane_axes).sum(0)
    piece = exchange(copies(piece, last), line_axes).sum(0)
    packed = exchange(copies(piece, first), plane_axes)

    send, inverse, stiff = solve(packed, near)
    rotated = unpack(exchange(send, MODE)).reshape(basis.shape)
    high = lax.Precision.HIGHEST
    reduced = jnp.dot(jnp.dot(inverse, stiff, precision=high), inverse.T, precision=high)
    return rotated, reduced


def solution(mesh):
    modes, slabs = mesh.devices.shape
    half = 2 if slabs % 4 == 0 else 1
    inner = Mesh(mesh.devices.reshape(modes // 2, 2, half, slabs // half), MODE + SPACE)
    field = P(MODE, None, SPACE, None, None)
    return jax.shard_map(
        per_device,
        mesh=inner,
        in_specs=(field, P(SPACE, None, None)),
        out_specs=(field, P()),
        check_vma=False,
    )
```

```python
import functools
import math

import jax
import jax.numpy as jnp
import numpy as np
from jax import lax
from jax.experimental import pallas as pl
from jax.experimental.pallas import tpu as pltpu
from jax.sharding import Mesh, PartitionSpec as P

VMEM = pltpu.VMEM
MODE = ("x", "yl")
SPACE = ("yh", "z", "core")
F32 = jnp.float32
BF16 = jnp.bfloat16


def hex_matrices():
    poisson = 0.3
    lame_first = poisson / ((1.0 + poisson) * (1.0 - 2.0 * poisson))
    shear = 1.0 / (2.0 * (1.0 + poisson))
    elastic = np.zeros((6, 6))
    elastic[:3, :3] = lame_first
    for number in range(3):
        elastic[number, number] += 2.0 * shear
        elastic[number + 3, number + 3] = shear
    points = [0.5 - 0.5 / math.sqrt(3.0), 0.5 + 0.5 / math.sqrt(3.0)]
    corners = [(a, b, c) for a in (0, 1) for b in (0, 1) for c in (0, 1)]
    stiff = np.zeros((24, 24))
    for point_x in points:
        for point_y in points:
            for point_z in points:
                strain = np.zeros((6, 24))
                for number, corner in enumerate(corners):
                    shape_x = point_x if corner[0] else 1.0 - point_x
                    shape_y = point_y if corner[1] else 1.0 - point_y
                    shape_z = point_z if corner[2] else 1.0 - point_z
                    deriv_x = (2.0 * corner[0] - 1.0) * shape_y * shape_z
                    deriv_y = shape_x * (2.0 * corner[1] - 1.0) * shape_z
                    deriv_z = shape_x * shape_y * (2.0 * corner[2] - 1.0)
                    strain[0, 3 * number] = deriv_x
                    strain[1, 3 * number + 1] = deriv_y
                    strain[2, 3 * number + 2] = deriv_z
                    strain[3, 3 * number] = deriv_y
                    strain[3, 3 * number + 1] = deriv_x
                    strain[4, 3 * number + 1] = deriv_z
                    strain[4, 3 * number + 2] = deriv_y
                    strain[5, 3 * number] = deriv_z
                    strain[5, 3 * number + 2] = deriv_x
                stiff += strain.T @ elastic @ strain / 8.0
    line = np.array([[1.0 / 3.0, 1.0 / 6.0], [1.0 / 6.0, 1.0 / 3.0]])
    mass = np.kron(np.kron(line, line), line)
    return stiff, mass


def factors():
    stiff, mass = hex_matrices()
    pair = np.array([[1.0, 1.0], [-1.0, 1.0]])
    modes = np.kron(np.kron(pair, pair), pair)
    mass_weight = np.sqrt(np.diag(modes @ mass @ modes.T) / 64.0)
    both = np.kron(modes, np.eye(3))
    blocks = both @ stiff @ both.T / 64.0
    rows = []
    for label in range(8):
        index = [(label ^ (4 >> comp)) * 3 + comp for comp in range(3)]
        block = blocks[np.ix_(index, index)].copy()
        for k in range(3):
            if block[k, k] > 1e-9:
                row = block[k] / math.sqrt(block[k, k])
                rows.append([(index[b], float(row[b])) for b in range(3) if abs(row[b]) > 1e-9])
                block -= np.outer(row, row)
        assert np.abs(block).max() < 1e-9
    return mass_weight, rows


def swap_blocks(vectors):
    block = lax.broadcasted_iota(jnp.int32, vectors[0].shape, 1) // 16
    vectors = [pltpu.roll(v, 16 * k, 1) if k else v for k, v in enumerate(vectors)]
    for step in (1, 2, 4):
        moved = (block & step) != 0
        vectors = [jnp.where(moved, vectors[(k + step) % 8], vectors[k]) for k in range(8)]
    return [pltpu.roll(vectors[-k % 8], 128 - 16 * k, 1) if k else vectors[0] for k in range(8)]


def slot_of(comp, half):
    return comp * 2 + half


def edge_lane(plane, comp, half):
    return half * 6 + plane * 3 + comp


def turned(chunk, turn):
    return chunk + turn if chunk % 2 == 0 else chunk - turn


def pack_body(turn_ref, x_ref, out0_ref, out1_ref):
    outs = (out0_ref, out1_ref)
    turn = turn_ref[0]
    for plane in range(2):
        for comp in range(3):
            first = (comp * 2 + plane) * 16
            lines = jnp.swapaxes(x_ref[:, first : first + 16, :], 0, 1)
            for half in range(2):
                parts = swap_blocks([lines[2 * k + half] for k in range(8)])
                for chunk in range(8):
                    outs[plane][turned(chunk, turn), slot_of(comp, half)] = parts[chunk]
    within = lax.broadcasted_iota(jnp.int32, (24, 128), 1) % 16
    for chunk in range(8):
        edge = jnp.zeros((24, 128), F32)
        for plane in range(2):
            for comp in range(3):
                for half in range(2):
                    lane = edge_lane(plane, comp, half)
                    value = outs[plane][turned((chunk + 1) % 8, turn), slot_of(comp, half)]
                    edge = jnp.where(within == lane, pltpu.roll(value, lane, 1), edge)
        out0_ref[turned(chunk, turn), 6] = edge


def pack(turn, basis):
    return pl.pallas_call(
        pack_body,
        out_shape=(
            jax.ShapeDtypeStruct((8, 7, 24, 128), F32),
            jax.ShapeDtypeStruct((8, 6, 24, 128), F32),
        ),
        in_specs=[pl.BlockSpec(memory_space=pltpu.SMEM), pl.BlockSpec(memory_space=VMEM)],
        out_specs=[pl.BlockSpec(memory_space=VMEM)] * 2,
        compiler_params=pltpu.CompilerParams(vmem_limit_bytes=12 * 2**20),
        name="pack",
    )(turn, basis.reshape(24, 96, 128))


def gram_body(scale, layer, first_ref, second_ref, edge_ref, w_ref, *rest):
    if layer == 0:
        before_ref, (out_ref, mass_ref, stiff_ref) = None, rest
        places = ((first_ref, first_ref, 0), (second_ref, first_ref, 1))
    else:
        before_ref, out_ref, mass_ref, stiff_ref = rest
        places = ((first_ref, edge_ref, 1), (second_ref, second_ref, 0))
    mass_weight, stiff_rows = factors()
    columns = 192
    last = lax.broadcasted_iota(jnp.int32, (16, 128), 1) % 16 == 15

    def read(ref, q, g, slot):
        parts = []
        for n in (2 * g, 2 * g + 1):
            t = n % 3
            parts.append(ref[2 * q + n // 3, slot, 8 * t : 8 * t + 8, :])
        return jnp.concatenate(parts, axis=0)

    def step(q, carry):
        for g in range(3):
            modes = {}
            edges = [read(edge, q, g, 6) for _, edge, _ in places]
            for comp in range(3):
                faces = {}
                for a, (ref, _, plane) in enumerate(places):
                    lines = {}
                    for half in range(2):
                        here = read(ref, q, g, slot_of(comp, half))
                        edge = pltpu.roll(edges[a], 15 - edge_lane(plane, comp, half), 1)
                        there = jnp.where(last, edge, pltpu.roll(here, 127, 1))
                        lines[half, 0] = here + there
                        lines[half, 1] = there - here
                    for pc in range(2):
                        even, odd = lines[0, pc], lines[1, pc]
                        following = pltpu.roll(even, 112, 1)
                        faces[a, 0, 0, pc] = odd + even
                        faces[a, 0, 1, pc] = odd - even
                        faces[a, 1, 0, pc] = following + odd
                        faces[a, 1, 1, pc] = following - odd
                for half in range(2):
                    for pb in range(2):
                        for pc in range(2):
                            low, high = faces[0, half, pb, pc], faces[1, half, pb, pc]
                            modes[half, (2 * pb + pc) * 3 + comp] = high + low
                            modes[half, (4 + 2 * pb + pc) * 3 + comp] = high - low
            start = pl.multiple_of(q * 48 + g * 16, 16)

            def put(ref, slot, value):
                high = value.astype(BF16)
                low = (value - high.astype(F32)).astype(BF16)
                ref[pl.ds(start, 16), slot * 128 : slot * 128 + 128] = high
                ref[pl.ds(columns + start, 16), slot * 128 : slot * 128 + 128] = low

            for half in range(2):
                root = w_ref[0, layer, pl.ds(half, 1), :]
                cubed = w_ref[1, layer, pl.ds(half, 1), :]
                for mode in range(24):
                    value = modes[half, mode] * (root * float(mass_weight[mode // 3]))
                    put(mass_ref, 24 * half + mode, value)
                for number, row in enumerate(stiff_rows):
                    total = None
                    for mode, coef in row:
                        term = modes[half, mode] * (cubed * coef)
                        total = term if total is None else total + term
                    put(stiff_ref, len(stiff_rows) * half + number, total)
        return carry

    lax.fori_loop(0, 4, step, 0)

    def whole(ref):
        both = lax.dot_general(
            ref[...], ref[:columns, :], (((1,), (1,)), ((), ())), preferred_element_type=F32
        )
        cross = both[columns:, :]
        return (both[:columns, :] + cross + cross.T) * scale

    mass, stiff = whole(mass_ref), whole(stiff_ref)
    row = lax.broadcasted_iota(jnp.int32, (columns, columns), 0)
    col = lax.broadcasted_iota(jnp.int32, (columns, columns), 1)
    mixed = jnp.where(row >= col, stiff, mass)
    diagonal = jnp.sum(jnp.where(row == col, mass, 0.0), axis=1, keepdims=True)
    out_ref[:columns, :] = mixed[:, :128]
    out_ref[columns:, :64] = mixed[:, 128:]
    out_ref[columns:, 64:] = jnp.broadcast_to(diagonal, (columns, 64))
    if before_ref is not None:
        out_ref[...] += before_ref[...]


def gram(layer, first, second, edge, weights, scale, before=()):
    stiff = len(factors()[1])
    return pl.pallas_call(
        functools.partial(gram_body, scale, layer),
        out_shape=jax.ShapeDtypeStruct((384, 128), F32),
        in_specs=[pl.BlockSpec(memory_space=VMEM)] * (4 + len(before)),
        out_specs=pl.BlockSpec(memory_space=VMEM),
        scratch_shapes=[
            VMEM((384, 2 * 24 * 128), BF16),
            VMEM((384, 2 * stiff * 128), BF16),
        ],
        compiler_params=pltpu.CompilerParams(vmem_limit_bytes=20 * 2**20),
        cost_estimate=pl.CostEstimate(flops=3 * 10**9, bytes_accessed=3 * 10**6, transcendentals=0),
        name="gram",
    )(first, second, edge, weights, *before)


def dot32(a, b, contract=((1,), (0,))):
    return lax.dot_general(
        a, b, (contract, ((), ())), precision=lax.Precision.HIGHEST, preferred_element_type=F32
    )


def eliminate(block, first, size):
    groups = size // 8
    sub = lax.broadcasted_iota(jnp.int32, (8, 128), 0)
    lane = lax.broadcasted_iota(jnp.int32, (8, 128), 1)
    spread = {}
    for k in range(size):
        for t in range(k // 8, groups):
            spread[k, t] = jnp.broadcast_to(block[8 * t : 8 * t + 8, first + k : first + k + 1], (8, 128))
    right = [jnp.where(lane == sub + 8 * t, 1.0, 0.0).astype(F32) for t in range(groups)]
    for i in range(size):
        at, inner = i // 8, i % 8
        inverse = 1.0 / spread[i, at][inner : inner + 1, :]
        factor = {t: spread[i, t] * inverse for t in range(at, groups)}
        factor[at] = jnp.where(sub > inner, factor[at], 0.0)
        for k in range(i + 1, size):
            entry = spread[i, k // 8][k % 8 : k % 8 + 1, :]
            for t in range(k // 8, groups):
                spread[k, t] = spread[k, t] - factor[t] * entry
        line = right[at][inner : inner + 1, :]
        for t in range(at, groups):
            right[t] = right[t] - factor[t] * line
    for t in range(groups):
        pivots = spread[8 * t, t]
        for inner in range(1, 8):
            pivots = jnp.where(sub == inner, spread[8 * t + inner, t], pivots)
        root = lax.rsqrt(pivots)
        right[t] = right[t] * (root * (1.5 - 0.5 * pivots * root * root))
    return jnp.concatenate(right, axis=0)[:, :size]


def split(value):
    high = value.astype(BF16)
    return high, (value - high.astype(F32)).astype(BF16)


def solve_body(g_ref, r0_ref, r1_ref, send_ref, inverse_ref, stiff_ref):
    columns, size = 192, 32
    packed = g_ref[...].reshape(384, 128)
    mixed = jnp.concatenate([packed[:columns], packed[columns:, :64]], axis=1)
    diagonal = packed[columns:, 64:65]
    row = lax.broadcasted_iota(jnp.int32, (columns, columns), 0)
    col = lax.broadcasted_iota(jnp.int32, (columns, columns), 1)
    other = mixed.T
    stiff_ref[...] = jnp.where(row >= col, mixed, other)
    mass = jnp.where(row < col, mixed, jnp.where(row == col, diagonal, other))
    unit = jnp.where(row == col, 1.0, 0.0).astype(F32)
    count = columns // size
    left = [mass[k * size : k * size + size] for k in range(count)]
    right = [unit[k * size : k * size + size] for k in range(count)]
    done = []
    for k in range(count):
        root = eliminate(left[k], k * size, size)
        line = dot32(root, left[k])
        if k + 1 < count:
            turned_line = line.T
            left[k + 1] = left[k + 1] - dot32(turned_line[(k + 1) * size : (k + 2) * size], line)
        ready = dot32(root, right[k])
        done.append(ready)
        if k + 1 < count:
            both = dot32(turned_line[(k + 1) * size :], ready)
            for i in range(k + 1, count):
                right[i] = right[i] - both[(i - k - 1) * size : (i - k) * size]
        if k + 2 < count:
            both = dot32(turned_line[(k + 2) * size :], line)
            for i in range(k + 2, count):
                left[i] = left[i] - both[(i - k - 2) * size : (i - k - 1) * size]
    inverse = jnp.concatenate(done, axis=0)
    inverse_ref[...] = inverse
    left_high, left_low = split(inverse)
    for plane, ref in enumerate((r0_ref, r1_ref)):
        for comp in range(3):
            sides = [ref[:, slot_of(comp, half)].reshape(columns, 128) for half in range(2)]
            right_high, right_low = split(jnp.concatenate(sides, axis=1))
            total = jnp.dot(left_high, right_high, preferred_element_type=F32)
            total += jnp.dot(left_high, right_low, preferred_element_type=F32)
            total += jnp.dot(left_low, right_high, preferred_element_type=F32)
            for half in range(2):
                part = total[:, 128 * half : 128 * half + 128].reshape(8, 24, 128)
                send_ref[:, plane * 6 + slot_of(comp, half)] = part


def solve(packed, first, second):
    return pl.pallas_call(
        solve_body,
        out_shape=(
            jax.ShapeDtypeStruct((8, 12, 24, 128), F32),
            jax.ShapeDtypeStruct((192, 192), F32),
            jax.ShapeDtypeStruct((192, 192), F32),
        ),
        in_specs=[pl.BlockSpec(memory_space=VMEM)] * 3,
        out_specs=[pl.BlockSpec(memory_space=VMEM)] * 3,
        compiler_params=pltpu.CompilerParams(vmem_limit_bytes=20 * 2**20),
        name="solve",
    )(packed, first, second)


def unpack_body(turn_ref, t_ref, out_ref, held_ref, sems):
    turn = turn_ref[0]
    copies_out = []
    for plane in range(2):
        for comp in range(3):
            lines = [None] * 16
            for half in range(2):
                slot = plane * 6 + slot_of(comp, half)
                lines[half::2] = swap_blocks([t_ref[turned(chunk, turn), slot] for chunk in range(8)])
            part = plane * 3 + comp
            held_ref[part] = jnp.swapaxes(jnp.stack(lines), 0, 1)
            rows = pl.ds((comp * 2 + plane) * 16, 16)
            copies_out.append(
                pltpu.make_async_copy(held_ref.at[part], out_ref.at[:, rows, :], sems.at[part])
            )
            copies_out[part].start()
    for copy in copies_out:
        copy.wait()


def unpack(turn, received):
    return pl.pallas_call(
        unpack_body,
        out_shape=jax.ShapeDtypeStruct((24, 96, 128), F32),
        in_specs=[pl.BlockSpec(memory_space=pltpu.SMEM), pl.BlockSpec(memory_space=VMEM)],
        out_specs=pl.BlockSpec(memory_space=pl.ANY),
        scratch_shapes=[VMEM((6, 24, 16, 128), F32), pltpu.SemaphoreType.DMA((6,))],
        compiler_params=pltpu.CompilerParams(vmem_limit_bytes=12 * 2**20),
        name="unpack",
    )(turn, received)


def exchange(value, axes):
    return lax.all_to_all(value, axes, 0, 0)


def copies(value, count):
    return jnp.broadcast_to(value[None], (count,) + value.shape)


def per_device(basis, density):
    chunks = lax.axis_size(MODE)
    slabs = lax.axis_size(SPACE)
    planes, width_y, width_z = basis.shape[2:]
    own = width_z // chunks
    scale = 1.0 / (3.0 * planes * width_y * width_z * slabs)
    turn = lax.axis_index("yh")
    chunk = lax.axis_index("x") * 2 + lax.abs(lax.axis_index("yl") - turn)
    density = lax.dynamic_slice_in_dim(density, chunk * own, own, axis=2)
    turn = turn.reshape(1)
    density = jnp.swapaxes(density.reshape(planes, width_y // 2, 2, own), 1, 2)
    density = density.reshape(planes, 2, width_y // 2 * own)
    root = jnp.sqrt(density)
    weights = jnp.stack([root, density * root])

    first, second = pack(turn, basis)
    first, second = exchange(first, MODE), exchange(second, MODE)
    half = slabs // lax.axis_size("yh")
    route = [
        (mode * slabs + slab, (mode ^ (slab % half == 0)) * slabs + slab - 1)
        for mode in range(chunks)
        for slab in range(1, slabs)
    ]
    above = lax.ppermute(first, MODE + SPACE, route)
    part = gram(0, first, second, first, weights, scale)
    part = gram(1, second, above, first, weights, scale, (part,))

    plane_axes = MODE + ("yh",)
    wide, deep = lax.axis_size(plane_axes), lax.axis_size("z")
    piece = exchange(part.reshape(wide, 384 // wide, 128), plane_axes).sum(0)
    piece = exchange(copies(piece, deep), "z").sum(0)
    piece = piece + lax.ppermute(piece, "core", [(0, 1), (1, 0)])
    packed = exchange(copies(piece, wide), plane_axes)

    send, inverse, stiff = solve(packed, first, second)
    rotated = unpack(turn, exchange(send, MODE)).reshape(basis.shape)
    high = lax.Precision.HIGHEST
    reduced = jnp.dot(jnp.dot(inverse, stiff, precision=high), inverse.T, precision=high)
    return rotated, reduced


def solution(mesh):
    modes, slabs = mesh.devices.shape
    half = 2 if slabs % 4 == 0 else 1
    inner = Mesh(mesh.devices.reshape(modes // 2, 2, half, slabs // half // 2, 2), MODE + SPACE)
    field = P(MODE, None, SPACE, None, None)
    return jax.shard_map(
        per_device,
        mesh=inner,
        in_specs=(field, P(SPACE, None, None)),
        out_specs=(field, P()),
        check_vma=False,
    )
```

```python
import functools
import math

import jax
import jax.numpy as jnp
import numpy as np
from jax import lax
from jax.experimental import pallas as pl
from jax.experimental.pallas import tpu as pltpu
from jax.sharding import Mesh, PartitionSpec as P

VMEM = pltpu.VMEM
MODE = ("x", "yl")
SPACE = ("yh", "z", "core")
F32 = jnp.float32
BF16 = jnp.bfloat16


def hex_matrices():
    poisson = 0.3
    lame_first = poisson / ((1.0 + poisson) * (1.0 - 2.0 * poisson))
    shear = 1.0 / (2.0 * (1.0 + poisson))
    elastic = np.zeros((6, 6))
    elastic[:3, :3] = lame_first
    for number in range(3):
        elastic[number, number] += 2.0 * shear
        elastic[number + 3, number + 3] = shear
    points = [0.5 - 0.5 / math.sqrt(3.0), 0.5 + 0.5 / math.sqrt(3.0)]
    corners = [(a, b, c) for a in (0, 1) for b in (0, 1) for c in (0, 1)]
    stiff = np.zeros((24, 24))
    for point_x in points:
        for point_y in points:
            for point_z in points:
                strain = np.zeros((6, 24))
                for number, corner in enumerate(corners):
                    shape_x = point_x if corner[0] else 1.0 - point_x
                    shape_y = point_y if corner[1] else 1.0 - point_y
                    shape_z = point_z if corner[2] else 1.0 - point_z
                    deriv_x = (2.0 * corner[0] - 1.0) * shape_y * shape_z
                    deriv_y = shape_x * (2.0 * corner[1] - 1.0) * shape_z
                    deriv_z = shape_x * shape_y * (2.0 * corner[2] - 1.0)
                    strain[0, 3 * number] = deriv_x
                    strain[1, 3 * number + 1] = deriv_y
                    strain[2, 3 * number + 2] = deriv_z
                    strain[3, 3 * number] = deriv_y
                    strain[3, 3 * number + 1] = deriv_x
                    strain[4, 3 * number + 1] = deriv_z
                    strain[4, 3 * number + 2] = deriv_y
                    strain[5, 3 * number] = deriv_z
                    strain[5, 3 * number + 2] = deriv_x
                stiff += strain.T @ elastic @ strain / 8.0
    line = np.array([[1.0 / 3.0, 1.0 / 6.0], [1.0 / 6.0, 1.0 / 3.0]])
    mass = np.kron(np.kron(line, line), line)
    return stiff, mass


def factors():
    stiff, mass = hex_matrices()
    pair = np.array([[1.0, 1.0], [-1.0, 1.0]])
    modes = np.kron(np.kron(pair, pair), pair)
    mass_weight = np.sqrt(np.diag(modes @ mass @ modes.T) / 64.0)
    both = np.kron(modes, np.eye(3))
    blocks = both @ stiff @ both.T / 64.0
    rows = []
    for label in range(8):
        index = [(label ^ (4 >> comp)) * 3 + comp for comp in range(3)]
        block = blocks[np.ix_(index, index)].copy()
        for k in range(3):
            if block[k, k] > 1e-9:
                row = block[k] / math.sqrt(block[k, k])
                rows.append([(index[b], float(row[b])) for b in range(3) if abs(row[b]) > 1e-9])
                block -= np.outer(row, row)
        assert np.abs(block).max() < 1e-9
    return mass_weight, rows


def swap_blocks(vectors):
    block = lax.broadcasted_iota(jnp.int32, vectors[0].shape, 1) // 16
    vectors = [pltpu.roll(v, 16 * k, 1) if k else v for k, v in enumerate(vectors)]
    for step in (1, 2, 4):
        moved = (block & step) != 0
        vectors = [jnp.where(moved, vectors[(k + step) % 8], vectors[k]) for k in range(8)]
    return [pltpu.roll(vectors[-k % 8], 128 - 16 * k, 1) if k else vectors[0] for k in range(8)]


def slot_of(comp, half):
    return comp * 2 + half


def edge_lane(plane, comp, half):
    return half * 6 + plane * 3 + comp


def turned(chunk, turn):
    return chunk + turn if chunk % 2 == 0 else chunk - turn


def place_lines(lines, comp, turn, out_ref):
    for half in range(2):
        parts = swap_blocks([lines[2 * k + half] for k in range(8)])
        for chunk in range(8):
            out_ref[turned(chunk, turn), slot_of(comp, half)] = parts[chunk]


def pack_first_body(turn_ref, x_ref, out_ref, held_ref, sems):
    turn = turn_ref[0]
    copies_in = []
    for part in range(6):
        rows = pl.ds((part % 3 * 2 + part // 3) * 16, 16)
        copies_in.append(
            pltpu.make_async_copy(x_ref.at[:, rows, :], held_ref.at[part], sems.at[part])
        )
        copies_in[part].start()
    within = lax.broadcasted_iota(jnp.int32, (24, 128), 1) % 16
    edges = [jnp.zeros((24, 128), F32)] * 8
    for plane in range(2):
        for comp in range(3):
            copies_in[plane * 3 + comp].wait()
            lines = jnp.swapaxes(held_ref[plane * 3 + comp], 0, 1)
            for half in range(2):
                lane = edge_lane(plane, comp, half)
                for k in range(8):
                    value = lines[2 * k + half]
                    value = pltpu.roll(value, lane, 1) if lane else value
                    edges[k] = jnp.where(within == lane, value, edges[k])
            if plane == 0:
                place_lines(lines, comp, turn, out_ref)
    edges = swap_blocks(edges)
    for chunk in range(8):
        out_ref[turned(chunk, turn), 6] = edges[(chunk + 1) % 8]


def pack_first(turn, basis):
    return pl.pallas_call(
        pack_first_body,
        out_shape=jax.ShapeDtypeStruct((8, 7, 24, 128), F32),
        in_specs=[pl.BlockSpec(memory_space=pltpu.SMEM), pl.BlockSpec(memory_space=pl.ANY)],
        out_specs=pl.BlockSpec(memory_space=VMEM),
        scratch_shapes=[VMEM((6, 24, 16, 128), F32), pltpu.SemaphoreType.DMA((6,))],
        compiler_params=pltpu.CompilerParams(vmem_limit_bytes=60 * 2**20),
        name="pack_first",
    )(turn, basis.reshape(24, 96, 128))


def pack_second_body(turn_ref, x_ref, out_ref):
    for comp in range(3):
        first = (comp * 2 + 1) * 16
        lines = jnp.swapaxes(x_ref[:, first : first + 16, :], 0, 1)
        place_lines(lines, comp, turn_ref[0], out_ref)


def pack_second(turn, basis):
    return pl.pallas_call(
        pack_second_body,
        out_shape=jax.ShapeDtypeStruct((8, 6, 24, 128), F32),
        in_specs=[pl.BlockSpec(memory_space=pltpu.SMEM), pl.BlockSpec(memory_space=VMEM)],
        out_specs=pl.BlockSpec(memory_space=VMEM),
        compiler_params=pltpu.CompilerParams(vmem_limit_bytes=12 * 2**20),
        name="pack_second",
    )(turn, basis.reshape(24, 96, 128))


def gram_body(scale, layer, first_ref, second_ref, w_ref, *rest):
    if layer == 0:
        before_ref = None
        out_ref, faces_ref, mass_ref, stiff_ref = rest
        places = ((0, first_ref, first_ref, 0), (1, second_ref, first_ref, 1))
    else:
        before_ref, out_ref, mass_ref, stiff_ref = rest
        faces_ref = first_ref
        places = ((1, second_ref, second_ref, 0),)
    mass_weight, stiff_rows = factors()
    columns = 192
    last = lax.broadcasted_iota(jnp.int32, (16, 128), 1) % 16 == 15

    def read(ref, q, g, slot):
        parts = []
        for n in (2 * g, 2 * g + 1):
            t = n % 3
            parts.append(ref[2 * q + n // 3, slot, 8 * t : 8 * t + 8, :])
        return jnp.concatenate(parts, axis=0)

    def step(q, carry):
        for g in range(3):
            modes = {}
            start = pl.multiple_of(q * 48 + g * 16, 16)
            edges = {a: read(edge, q, g, 6) for a, _, edge, _ in places}
            for comp in range(3):
                faces = {}
                for a, ref, _, plane in places:
                    lines = {}
                    for half in range(2):
                        here = read(ref, q, g, slot_of(comp, half))
                        edge = pltpu.roll(edges[a], 15 - edge_lane(plane, comp, half), 1)
                        there = jnp.where(last, edge, pltpu.roll(here, 127, 1))
                        lines[half, 0] = here + there
                        lines[half, 1] = there - here
                    for pc in range(2):
                        even, odd = lines[0, pc], lines[1, pc]
                        following = pltpu.roll(even, 112, 1)
                        faces[a, 0, 0, pc] = odd + even
                        faces[a, 0, 1, pc] = odd - even
                        faces[a, 1, 0, pc] = following + odd
                        faces[a, 1, 1, pc] = following - odd
                for half in range(2):
                    for pb in range(2):
                        for pc in range(2):
                            slot = (half * 4 + pb * 2 + pc) * 3 + comp
                            if layer == 0:
                                faces_ref[slot, pl.ds(start, 16), :] = faces[1, half, pb, pc]
                            else:
                                faces[0, half, pb, pc] = faces_ref[slot, pl.ds(start, 16), :]
                for half in range(2):
                    for pb in range(2):
                        for pc in range(2):
                            low, high = faces[0, half, pb, pc], faces[1, half, pb, pc]
                            modes[half, (2 * pb + pc) * 3 + comp] = high + low
                            modes[half, (4 + 2 * pb + pc) * 3 + comp] = high - low
            def put(ref, slot, value):
                high = value.astype(BF16)
                low = (value - high.astype(F32)).astype(BF16)
                ref[pl.ds(start, 16), slot * 128 : slot * 128 + 128] = high
                ref[pl.ds(columns + start, 16), slot * 128 : slot * 128 + 128] = low

            for half in range(2):
                root = w_ref[0, layer, pl.ds(half, 1), :]
                cubed = w_ref[1, layer, pl.ds(half, 1), :]
                for mode in range(24):
                    value = modes[half, mode] * (root * float(mass_weight[mode // 3]))
                    put(mass_ref, 24 * half + mode, value)
                for number, row in enumerate(stiff_rows):
                    total = None
                    for mode, coef in row:
                        term = modes[half, mode] * (cubed * coef)
                        total = term if total is None else total + term
                    put(stiff_ref, len(stiff_rows) * half + number, total)
        return carry

    lax.fori_loop(0, 4, step, 0)

    def halves(ref):
        both = lax.dot_general(
            ref[...], ref[:columns, :], (((1,), (1,)), ((), ())), preferred_element_type=F32
        )
        return both[:columns, :] + both[columns:, :], both[columns:, :]

    mass, mass_cross = halves(mass_ref)
    stiff, stiff_cross = halves(stiff_ref)
    row = lax.broadcasted_iota(jnp.int32, (columns, columns), 0)
    col = lax.broadcasted_iota(jnp.int32, (columns, columns), 1)
    cross = jnp.where(row <= col, stiff_cross, mass_cross)
    mixed = (jnp.where(row >= col, stiff, mass) + cross.T) * scale
    diagonal = jnp.where(row == col, mass + mass_cross, 0.0)
    diagonal = jnp.sum(diagonal, axis=1, keepdims=True) * scale
    out_ref[:columns, :] = mixed[:, :128]
    out_ref[columns:, :64] = mixed[:, 128:]
    out_ref[columns:, 64:] = jnp.broadcast_to(diagonal, (columns, 64))
    if before_ref is not None:
        out_ref[...] += before_ref[...]


def gram(layer, scale, operands):
    stiff = len(factors()[1])
    shapes = [jax.ShapeDtypeStruct((384, 128), F32)]
    if layer == 0:
        shapes.append(jax.ShapeDtypeStruct((24, 192, 128), F32))
    return pl.pallas_call(
        functools.partial(gram_body, scale, layer),
        out_shape=shapes,
        in_specs=[pl.BlockSpec(memory_space=VMEM)] * len(operands),
        out_specs=[pl.BlockSpec(memory_space=VMEM)] * len(shapes),
        scratch_shapes=[
            VMEM((384, 2 * 24 * 128), BF16),
            VMEM((384, 2 * stiff * 128), BF16),
        ],
        compiler_params=pltpu.CompilerParams(vmem_limit_bytes=20 * 2**20),
        cost_estimate=pl.CostEstimate(flops=3 * 10**9, bytes_accessed=3 * 10**6, transcendentals=0),
        name="gram",
    )(*operands)


def dot32(a, b, contract=((1,), (0,))):
    return lax.dot_general(
        a, b, (contract, ((), ())), precision=lax.Precision.HIGHEST, preferred_element_type=F32
    )


def eliminate(block, first, size):
    groups = size // 8
    sub = lax.broadcasted_iota(jnp.int32, (8, 128), 0)
    lane = lax.broadcasted_iota(jnp.int32, (8, 128), 1)
    spread = {}
    for k in range(size):
        for t in range(k // 8, groups):
            tile = (first + k) // 128 * 128
            index = jnp.full((8, 128), first + k - tile, jnp.int32)
            spread[k, t] = jnp.take_along_axis(
                block[8 * t : 8 * t + 8, tile : tile + 128], index, axis=1
            )
    right = [jnp.where(lane == sub + 8 * t, 1.0, 0.0).astype(F32) for t in range(groups)]
    for i in range(size):
        at, inner = i // 8, i % 8
        inverse = 1.0 / spread[i, at][inner : inner + 1, :]
        factor = {t: spread[i, t] * inverse for t in range(at, groups)}
        factor[at] = jnp.where(sub > inner, factor[at], 0.0)
        for k in range(i + 1, size):
            entry = spread[i, k // 8][k % 8 : k % 8 + 1, :]
            for t in range(k // 8, groups):
                spread[k, t] = spread[k, t] - factor[t] * entry
        line = right[at][inner : inner + 1, :]
        for t in range(at, groups):
            right[t] = right[t] - factor[t] * line
    for t in range(groups):
        pivots = spread[8 * t, t]
        for inner in range(1, 8):
            pivots = jnp.where(sub == inner, spread[8 * t + inner, t], pivots)
        root = lax.rsqrt(pivots)
        right[t] = right[t] * (root * (1.5 - 0.5 * pivots * root * root))
    return jnp.concatenate(right, axis=0)[:, :size]


def split(value):
    high = value.astype(BF16)
    return high, (value - high.astype(F32)).astype(BF16)


def solve_body(g_ref, r0_ref, r1_ref, send_ref, inverse_ref):
    columns, size = 192, 32
    packed = g_ref[...].reshape(384, 128)
    mixed = jnp.concatenate([packed[:columns], packed[columns:, :64]], axis=1)
    diagonal = packed[columns:, 64:65]
    row = lax.broadcasted_iota(jnp.int32, (columns, columns), 0)
    col = lax.broadcasted_iota(jnp.int32, (columns, columns), 1)
    other = mixed.T
    mass = jnp.where(row < col, mixed, jnp.where(row == col, diagonal, other))
    unit = jnp.where(row == col, 1.0, 0.0).astype(F32)
    count = columns // size
    mass = jnp.concatenate([mass, jnp.zeros((columns, 64), F32)], axis=1)
    left = [mass[k * size : k * size + size] for k in range(count)]
    right = [unit[k * size : k * size + size] for k in range(count)]
    done = []
    for k in range(count):
        root = eliminate(left[k], k * size, size)
        line = dot32(root, left[k])
        if k + 1 < count:
            turned_line = line.T
            left[k + 1] = left[k + 1] - dot32(turned_line[(k + 1) * size : (k + 2) * size], line)
        ready = dot32(root, right[k])
        done.append(ready)
        if k + 1 < count:
            both = dot32(turned_line[(k + 1) * size :], ready)
            for i in range(k + 1, count):
                right[i] = right[i] - both[(i - k - 1) * size : (i - k) * size]
        if k + 2 < count:
            both = dot32(turned_line[(k + 2) * size :], line)
            for i in range(k + 2, count):
                left[i] = left[i] - both[(i - k - 2) * size : (i - k - 1) * size]
    inverse = jnp.concatenate(done, axis=0)
    inverse_ref[...] = inverse
    left_high, left_low = split(inverse)
    for plane, ref in enumerate((r0_ref, r1_ref)):
        for comp in range(3):
            sides = [ref[:, slot_of(comp, half)].reshape(columns, 128) for half in range(2)]
            right_high, right_low = split(jnp.concatenate(sides, axis=1))
            total = jnp.dot(left_high, right_high, preferred_element_type=F32)
            total += jnp.dot(left_high, right_low, preferred_element_type=F32)
            total += jnp.dot(left_low, right_high, preferred_element_type=F32)
            for half in range(2):
                part = total[:, 128 * half : 128 * half + 128].reshape(8, 24, 128)
                send_ref[:, plane * 6 + slot_of(comp, half)] = part


def solve(packed, first, second):
    return pl.pallas_call(
        solve_body,
        out_shape=(
            jax.ShapeDtypeStruct((8, 12, 24, 128), F32),
            jax.ShapeDtypeStruct((192, 192), F32),
        ),
        in_specs=[pl.BlockSpec(memory_space=VMEM)] * 3,
        out_specs=[pl.BlockSpec(memory_space=VMEM)] * 2,
        compiler_params=pltpu.CompilerParams(vmem_limit_bytes=20 * 2**20),
        name="solve",
    )(packed, first, second)


def unpack_body(turn_ref, t_ref, out_ref, held_ref, sems):
    turn = turn_ref[0]
    copies_out = []
    for plane in range(2):
        for comp in range(3):
            lines = [None] * 16
            for half in range(2):
                slot = plane * 6 + slot_of(comp, half)
                lines[half::2] = swap_blocks([t_ref[turned(chunk, turn), slot] for chunk in range(8)])
            part = plane * 3 + comp
            held_ref[part] = jnp.swapaxes(jnp.stack(lines), 0, 1)
            rows = pl.ds((comp * 2 + plane) * 16, 16)
            copies_out.append(
                pltpu.make_async_copy(held_ref.at[part], out_ref.at[:, rows, :], sems.at[part])
            )
            copies_out[part].start()
    for copy in copies_out:
        copy.wait()


def unpack(turn, received):
    return pl.pallas_call(
        unpack_body,
        out_shape=jax.ShapeDtypeStruct((24, 96, 128), F32),
        in_specs=[pl.BlockSpec(memory_space=pltpu.SMEM), pl.BlockSpec(memory_space=VMEM)],
        out_specs=pl.BlockSpec(memory_space=pl.ANY),
        scratch_shapes=[VMEM((6, 24, 16, 128), F32), pltpu.SemaphoreType.DMA((6,))],
        compiler_params=pltpu.CompilerParams(vmem_limit_bytes=12 * 2**20),
        name="unpack",
    )(turn, received)


def exchange(value, axes):
    return lax.all_to_all(value, axes, 0, 0)


def copies(value, count):
    return jnp.broadcast_to(value[None], (count,) + value.shape)


def per_device(basis, density):
    chunks = lax.axis_size(MODE)
    slabs = lax.axis_size(SPACE)
    planes, width_y, width_z = basis.shape[2:]
    own = width_z // chunks
    scale = 1.0 / (3.0 * planes * width_y * width_z * slabs)
    turn = lax.axis_index("yh")
    chunk = lax.axis_index("x") * 2 + lax.abs(lax.axis_index("yl") - turn)
    density = lax.dynamic_slice_in_dim(density, chunk * own, own, axis=2)
    turn = turn.reshape(1)
    density = jnp.swapaxes(density.reshape(planes, width_y // 2, 2, own), 1, 2)
    density = density.reshape(planes, 2, width_y // 2 * own)
    root = jnp.sqrt(density)
    weights = jnp.stack([root, density * root])

    first = exchange(pack_first(turn, basis), MODE)
    second = exchange(pack_second(turn, basis), MODE)
    half = slabs // lax.axis_size("yh")
    route = [
        (mode * slabs + slab, (mode ^ (slab % half == 0)) * slabs + slab - 1)
        for mode in range(chunks)
        for slab in range(1, slabs)
    ]
    above = lax.ppermute(first, MODE + SPACE, route)
    part, faces = gram(0, scale, (first, second, weights))
    (part,) = gram(1, scale, (faces, above, weights, part))

    plane_axes = MODE + ("yh",)
    wide, deep = lax.axis_size(plane_axes), lax.axis_size("z")
    piece = exchange(part.reshape(wide, 384 // wide, 128), plane_axes).sum(0)
    piece = piece + lax.ppermute(piece, "core", [(0, 1), (1, 0)])
    piece = exchange(copies(piece, deep), "z").sum(0)
    packed = exchange(copies(piece, wide), plane_axes)

    send, inverse = solve(packed, first, second)
    rotated = unpack(turn, exchange(send, MODE)).reshape(basis.shape)
    high = lax.Precision.HIGHEST
    packed = packed.reshape(384, 128)
    stiff = jnp.concatenate([packed[:192], packed[192:, :64]], axis=1)
    stiff = jnp.tril(stiff) + jnp.tril(stiff, -1).T
    reduced = jnp.dot(jnp.dot(inverse, stiff, precision=high), inverse.T, precision=high)
    return rotated, reduced


def solution(mesh):
    modes, slabs = mesh.devices.shape
    half = 2 if slabs % 4 == 0 else 1
    inner = Mesh(mesh.devices.reshape(modes // 2, 2, half, slabs // half // 2, 2), MODE + SPACE)
    field = P(MODE, None, SPACE, None, None)
    return jax.shard_map(
        per_device,
        mesh=inner,
        in_specs=(field, P(SPACE, None, None)),
        out_specs=(field, P()),
        check_vma=False,
    )
```

```python
import functools
import math

import jax
import jax.numpy as jnp
import numpy as np
from jax import lax
from jax.experimental import pallas as pl
from jax.experimental.pallas import tpu as pltpu
from jax.sharding import Mesh, PartitionSpec as P

VMEM = pltpu.VMEM
MODE = ("x", "yl")
SPACE = ("yh", "z", "core")
F32 = jnp.float32
BF16 = jnp.bfloat16


def hex_matrices():
    poisson = 0.3
    lame_first = poisson / ((1.0 + poisson) * (1.0 - 2.0 * poisson))
    shear = 1.0 / (2.0 * (1.0 + poisson))
    elastic = np.zeros((6, 6))
    elastic[:3, :3] = lame_first
    for number in range(3):
        elastic[number, number] += 2.0 * shear
        elastic[number + 3, number + 3] = shear
    points = [0.5 - 0.5 / math.sqrt(3.0), 0.5 + 0.5 / math.sqrt(3.0)]
    corners = [(a, b, c) for a in (0, 1) for b in (0, 1) for c in (0, 1)]
    stiff = np.zeros((24, 24))
    for point_x in points:
        for point_y in points:
            for point_z in points:
                strain = np.zeros((6, 24))
                for number, corner in enumerate(corners):
                    shape_x = point_x if corner[0] else 1.0 - point_x
                    shape_y = point_y if corner[1] else 1.0 - point_y
                    shape_z = point_z if corner[2] else 1.0 - point_z
                    deriv_x = (2.0 * corner[0] - 1.0) * shape_y * shape_z
                    deriv_y = shape_x * (2.0 * corner[1] - 1.0) * shape_z
                    deriv_z = shape_x * shape_y * (2.0 * corner[2] - 1.0)
                    strain[0, 3 * number] = deriv_x
                    strain[1, 3 * number + 1] = deriv_y
                    strain[2, 3 * number + 2] = deriv_z
                    strain[3, 3 * number] = deriv_y
                    strain[3, 3 * number + 1] = deriv_x
                    strain[4, 3 * number + 1] = deriv_z
                    strain[4, 3 * number + 2] = deriv_y
                    strain[5, 3 * number] = deriv_z
                    strain[5, 3 * number + 2] = deriv_x
                stiff += strain.T @ elastic @ strain / 8.0
    line = np.array([[1.0 / 3.0, 1.0 / 6.0], [1.0 / 6.0, 1.0 / 3.0]])
    mass = np.kron(np.kron(line, line), line)
    return stiff, mass


def factors():
    stiff, mass = hex_matrices()
    pair = np.array([[1.0, 1.0], [-1.0, 1.0]])
    modes = np.kron(np.kron(pair, pair), pair)
    mass_weight = np.sqrt(np.diag(modes @ mass @ modes.T) / 64.0)
    both = np.kron(modes, np.eye(3))
    blocks = both @ stiff @ both.T / 64.0
    rows = []
    for label in range(8):
        index = [(label ^ (4 >> comp)) * 3 + comp for comp in range(3)]
        block = blocks[np.ix_(index, index)].copy()
        for k in range(3):
            if block[k, k] > 1e-9:
                row = block[k] / math.sqrt(block[k, k])
                rows.append([(index[b], float(row[b])) for b in range(3) if abs(row[b]) > 1e-9])
                block -= np.outer(row, row)
        assert np.abs(block).max() < 1e-9
    return mass_weight, rows


def swap_blocks(vectors):
    block = lax.broadcasted_iota(jnp.int32, vectors[0].shape, 1) // 16
    vectors = [pltpu.roll(v, 16 * k, 1) if k else v for k, v in enumerate(vectors)]
    for step in (1, 2, 4):
        moved = (block & step) != 0
        vectors = [jnp.where(moved, vectors[(k + step) % 8], vectors[k]) for k in range(8)]
    return [pltpu.roll(vectors[-k % 8], 128 - 16 * k, 1) if k else vectors[0] for k in range(8)]


def slot_of(comp, half):
    return comp * 2 + half


def edge_lane(plane, comp, half):
    return half * 6 + plane * 3 + comp


def turned(chunk, turn):
    return chunk + turn if chunk % 2 == 0 else chunk - turn


def place_lines(lines, comp, turn, out_ref):
    for half in range(2):
        parts = swap_blocks([lines[2 * k + half] for k in range(8)])
        for chunk in range(8):
            out_ref[turned(chunk, turn), slot_of(comp, half)] = parts[chunk]


def pack_first_body(turn_ref, x_ref, out_ref, held_ref, sems):
    turn = turn_ref[0]
    copies_in = []
    for part in range(6):
        rows = pl.ds((part % 3 * 2 + part // 3) * 16, 16)
        copies_in.append(
            pltpu.make_async_copy(x_ref.at[:, rows, :], held_ref.at[part], sems.at[part])
        )
        copies_in[part].start()
    within = lax.broadcasted_iota(jnp.int32, (24, 128), 1) % 16
    edges = [jnp.zeros((24, 128), F32)] * 8
    for plane in range(2):
        for comp in range(3):
            copies_in[plane * 3 + comp].wait()
            lines = jnp.swapaxes(held_ref[plane * 3 + comp], 0, 1)
            for half in range(2):
                lane = edge_lane(plane, comp, half)
                for k in range(8):
                    value = lines[2 * k + half]
                    value = pltpu.roll(value, lane, 1) if lane else value
                    edges[k] = jnp.where(within == lane, value, edges[k])
            if plane == 0:
                place_lines(lines, comp, turn, out_ref)
    edges = swap_blocks(edges)
    for chunk in range(8):
        out_ref[turned(chunk, turn), 6] = edges[(chunk + 1) % 8]


def pack_first(turn, basis):
    return pl.pallas_call(
        pack_first_body,
        out_shape=jax.ShapeDtypeStruct((8, 7, 24, 128), F32),
        in_specs=[pl.BlockSpec(memory_space=pltpu.SMEM), pl.BlockSpec(memory_space=pl.ANY)],
        out_specs=pl.BlockSpec(memory_space=VMEM),
        scratch_shapes=[VMEM((6, 24, 16, 128), F32), pltpu.SemaphoreType.DMA((6,))],
        compiler_params=pltpu.CompilerParams(vmem_limit_bytes=60 * 2**20),
        name="pack_first",
    )(turn, basis.reshape(24, 96, 128))


def pack_second_body(turn_ref, x_ref, out_ref):
    for comp in range(3):
        first = (comp * 2 + 1) * 16
        lines = jnp.swapaxes(x_ref[:, first : first + 16, :], 0, 1)
        place_lines(lines, comp, turn_ref[0], out_ref)


def pack_second(turn, basis):
    return pl.pallas_call(
        pack_second_body,
        out_shape=jax.ShapeDtypeStruct((8, 6, 24, 128), F32),
        in_specs=[pl.BlockSpec(memory_space=pltpu.SMEM), pl.BlockSpec(memory_space=VMEM)],
        out_specs=pl.BlockSpec(memory_space=VMEM),
        compiler_params=pltpu.CompilerParams(vmem_limit_bytes=12 * 2**20),
        name="pack_second",
    )(turn, basis.reshape(24, 96, 128))


def gram_body(scale, layer, first_ref, second_ref, w_ref, *rest):
    if layer == 0:
        before_ref = None
        out_ref, faces_ref, mass_ref, stiff_ref = rest
        places = ((0, first_ref, first_ref, 0), (1, second_ref, first_ref, 1))
    else:
        before_ref, out_ref, mass_ref, stiff_ref = rest
        faces_ref = first_ref
        places = ((1, second_ref, second_ref, 0),)
    mass_weight, stiff_rows = factors()
    columns = 192
    last = lax.broadcasted_iota(jnp.int32, (16, 128), 1) % 16 == 15

    def read(ref, q, g, slot):
        parts = []
        for n in (2 * g, 2 * g + 1):
            t = n % 3
            parts.append(ref[2 * q + n // 3, slot, 8 * t : 8 * t + 8, :])
        return jnp.concatenate(parts, axis=0)

    def step(q, carry):
        for g in range(3):
            modes = {}
            start = pl.multiple_of(q * 48 + g * 16, 16)
            edges = {a: read(edge, q, g, 6) for a, _, edge, _ in places}
            for comp in range(3):
                faces = {}
                for a, ref, _, plane in places:
                    lines = {}
                    for half in range(2):
                        here = read(ref, q, g, slot_of(comp, half))
                        edge = pltpu.roll(edges[a], 15 - edge_lane(plane, comp, half), 1)
                        there = jnp.where(last, edge, pltpu.roll(here, 127, 1))
                        lines[half, 0] = here + there
                        lines[half, 1] = there - here
                    for pc in range(2):
                        even, odd = lines[0, pc], lines[1, pc]
                        following = pltpu.roll(even, 112, 1)
                        faces[a, 0, 0, pc] = odd + even
                        faces[a, 0, 1, pc] = odd - even
                        faces[a, 1, 0, pc] = following + odd
                        faces[a, 1, 1, pc] = following - odd
                for half in range(2):
                    for pb in range(2):
                        for pc in range(2):
                            slot = (half * 4 + pb * 2 + pc) * 3 + comp
                            if layer == 0:
                                faces_ref[slot, pl.ds(start, 16), :] = faces[1, half, pb, pc]
                            else:
                                faces[0, half, pb, pc] = faces_ref[slot, pl.ds(start, 16), :]
                for half in range(2):
                    for pb in range(2):
                        for pc in range(2):
                            low, high = faces[0, half, pb, pc], faces[1, half, pb, pc]
                            modes[half, (2 * pb + pc) * 3 + comp] = high + low
                            modes[half, (4 + 2 * pb + pc) * 3 + comp] = high - low
            def put(ref, slot, value):
                high = value.astype(BF16)
                low = (value - high.astype(F32)).astype(BF16)
                ref[pl.ds(start, 16), slot * 128 : slot * 128 + 128] = high
                ref[pl.ds(columns + start, 16), slot * 128 : slot * 128 + 128] = low

            for half in range(2):
                root = w_ref[0, layer, pl.ds(half, 1), :]
                cubed = w_ref[1, layer, pl.ds(half, 1), :]
                for mode in range(24):
                    value = modes[half, mode] * (root * float(mass_weight[mode // 3]))
                    put(mass_ref, 24 * half + mode, value)
                for number, row in enumerate(stiff_rows):
                    total = None
                    for mode, coef in row:
                        term = modes[half, mode] * (cubed * coef)
                        total = term if total is None else total + term
                    put(stiff_ref, len(stiff_rows) * half + number, total)
        return carry

    lax.fori_loop(0, 4, step, 0)

    def halves(ref):
        both = lax.dot_general(
            ref[...], ref[:columns, :], (((1,), (1,)), ((), ())), preferred_element_type=F32
        )
        return both[:columns, :] + both[columns:, :], both[columns:, :]

    mass, mass_cross = halves(mass_ref)
    stiff, stiff_cross = halves(stiff_ref)
    row = lax.broadcasted_iota(jnp.int32, (columns, columns), 0)
    col = lax.broadcasted_iota(jnp.int32, (columns, columns), 1)
    cross = jnp.where(row <= col, stiff_cross, mass_cross)
    mixed = (jnp.where(row >= col, stiff, mass) + cross.T) * scale
    diagonal = jnp.where(row == col, mass + mass_cross, 0.0)
    diagonal = jnp.sum(diagonal, axis=1, keepdims=True) * scale
    out_ref[:columns, :] = mixed[:, :128]
    out_ref[columns:, :64] = mixed[:, 128:]
    out_ref[columns:, 64:] = jnp.broadcast_to(diagonal, (columns, 64))
    if before_ref is not None:
        out_ref[...] += before_ref[...]


def gram(layer, scale, operands):
    stiff = len(factors()[1])
    shapes = [jax.ShapeDtypeStruct((384, 128), F32)]
    if layer == 0:
        shapes.append(jax.ShapeDtypeStruct((24, 192, 128), F32))
    return pl.pallas_call(
        functools.partial(gram_body, scale, layer),
        out_shape=shapes,
        in_specs=[pl.BlockSpec(memory_space=VMEM)] * len(operands),
        out_specs=[pl.BlockSpec(memory_space=VMEM)] * len(shapes),
        scratch_shapes=[
            VMEM((384, 2 * 24 * 128), BF16),
            VMEM((384, 2 * stiff * 128), BF16),
        ],
        compiler_params=pltpu.CompilerParams(vmem_limit_bytes=20 * 2**20),
        cost_estimate=pl.CostEstimate(flops=3 * 10**9, bytes_accessed=3 * 10**6, transcendentals=0),
        name="gram",
    )(*operands)


def dot32(a, b, contract=((1,), (0,))):
    return lax.dot_general(
        a, b, (contract, ((), ())), precision=lax.Precision.HIGHEST, preferred_element_type=F32
    )


def eliminate(block, first, size):
    groups = size // 8
    sub = lax.broadcasted_iota(jnp.int32, (8, 128), 0)
    lane = lax.broadcasted_iota(jnp.int32, (8, 128), 1)
    spread = {}
    for k in range(size):
        for t in range(k // 8, groups):
            tile = (first + k) // 128 * 128
            index = jnp.full((8, 128), first + k - tile, jnp.int32)
            spread[k, t] = jnp.take_along_axis(
                block[8 * t : 8 * t + 8, tile : tile + 128], index, axis=1
            )
    right = [jnp.where(lane == sub + 8 * t, 1.0, 0.0).astype(F32) for t in range(groups)]
    for i in range(size):
        at, inner = i // 8, i % 8
        inverse = 1.0 / spread[i, at][inner : inner + 1, :]
        factor = {t: spread[i, t] * inverse for t in range(at, groups)}
        factor[at] = jnp.where(sub > inner, factor[at], 0.0)
        for k in range(i + 1, size):
            entry = spread[i, k // 8][k % 8 : k % 8 + 1, :]
            for t in range(k // 8, groups):
                spread[k, t] = spread[k, t] - factor[t] * entry
        line = right[at][inner : inner + 1, :]
        for t in range(at, groups):
            right[t] = right[t] - factor[t] * line
    for t in range(groups):
        pivots = spread[8 * t, t]
        for inner in range(1, 8):
            pivots = jnp.where(sub == inner, spread[8 * t + inner, t], pivots)
        root = lax.rsqrt(pivots)
        right[t] = right[t] * (root * (1.5 - 0.5 * pivots * root * root))
    return jnp.concatenate(right, axis=0)[:, :size]


def split(value):
    high = value.astype(BF16)
    return high, (value - high.astype(F32)).astype(BF16)


def solve_body(g_ref, r0_ref, r1_ref, send_ref, inverse_ref, held_ref, sems):
    copies_out = []
    columns, size = 192, 32
    packed = g_ref[...].reshape(384, 128)
    mixed = jnp.concatenate([packed[:columns], packed[columns:, :64]], axis=1)
    diagonal = packed[columns:, 64:65]
    row = lax.broadcasted_iota(jnp.int32, (columns, columns), 0)
    col = lax.broadcasted_iota(jnp.int32, (columns, columns), 1)
    other = mixed.T
    mass = jnp.where(row < col, mixed, jnp.where(row == col, diagonal, other))
    unit = jnp.where(row == col, 1.0, 0.0).astype(F32)
    count = columns // size
    mass = jnp.concatenate([mass, jnp.zeros((columns, 64), F32)], axis=1)
    left = [mass[k * size : k * size + size] for k in range(count)]
    right = [unit[k * size : k * size + size] for k in range(count)]
    done = []
    for k in range(count):
        root = eliminate(left[k], k * size, size)
        line = dot32(root, left[k])
        if k + 1 < count:
            turned_line = line.T
            left[k + 1] = left[k + 1] - dot32(turned_line[(k + 1) * size : (k + 2) * size], line)
        ready = dot32(root, right[k])
        done.append(ready)
        if k + 1 < count:
            both = dot32(turned_line[(k + 1) * size :], ready)
            for i in range(k + 1, count):
                right[i] = right[i] - both[(i - k - 1) * size : (i - k) * size]
        if k + 2 < count:
            both = dot32(turned_line[(k + 2) * size :], line)
            for i in range(k + 2, count):
                left[i] = left[i] - both[(i - k - 2) * size : (i - k - 1) * size]
    inverse = jnp.concatenate(done, axis=0)
    inverse_ref[...] = inverse
    left_high, left_low = split(inverse)
    for plane, ref in enumerate((r0_ref, r1_ref)):
        for comp in range(3):
            sides = [ref[:, slot_of(comp, half)].reshape(columns, 128) for half in range(2)]
            right_high, right_low = split(jnp.concatenate(sides, axis=1))
            total = jnp.dot(left_high, right_high, preferred_element_type=F32)
            total += jnp.dot(left_high, right_low, preferred_element_type=F32)
            total += jnp.dot(left_low, right_high, preferred_element_type=F32)
            for half in range(2):
                part = total[:, 128 * half : 128 * half + 128].reshape(8, 24, 128)
                held_ref[plane * 3 + comp, :, half] = part
            at = plane * 3 + comp
            target = send_ref.at[:, pl.ds(2 * at, 2)]
            copies_out.append(pltpu.make_async_copy(held_ref.at[at], target, sems.at[at]))
            copies_out[at].start()
    for copy in copies_out:
        copy.wait()


def solve(packed, first, second):
    return pl.pallas_call(
        solve_body,
        out_shape=(
            jax.ShapeDtypeStruct((8, 12, 24, 128), F32),
            jax.ShapeDtypeStruct((192, 192), F32),
        ),
        in_specs=[pl.BlockSpec(memory_space=VMEM)] * 3,
        out_specs=[pl.BlockSpec(memory_space=pl.ANY), pl.BlockSpec(memory_space=VMEM)],
        scratch_shapes=[VMEM((6, 8, 2, 24, 128), F32), pltpu.SemaphoreType.DMA((6,))],
        compiler_params=pltpu.CompilerParams(vmem_limit_bytes=20 * 2**20),
        name="solve",
    )(packed, first, second)


def unpack_body(turn_ref, t_ref, out_ref, held_ref, sems):
    turn = turn_ref[0]
    copies_out = []
    for plane in range(2):
        for comp in range(3):
            lines = [None] * 16
            for half in range(2):
                slot = plane * 6 + slot_of(comp, half)
                lines[half::2] = swap_blocks([t_ref[turned(chunk, turn), slot] for chunk in range(8)])
            part = plane * 3 + comp
            held_ref[part] = jnp.swapaxes(jnp.stack(lines), 0, 1)
            rows = pl.ds((comp * 2 + plane) * 16, 16)
            copies_out.append(
                pltpu.make_async_copy(held_ref.at[part], out_ref.at[:, rows, :], sems.at[part])
            )
            copies_out[part].start()
    for copy in copies_out:
        copy.wait()


def unpack(turn, received):
    return pl.pallas_call(
        unpack_body,
        out_shape=jax.ShapeDtypeStruct((24, 96, 128), F32),
        in_specs=[pl.BlockSpec(memory_space=pltpu.SMEM), pl.BlockSpec(memory_space=VMEM)],
        out_specs=pl.BlockSpec(memory_space=pl.ANY),
        scratch_shapes=[VMEM((6, 24, 16, 128), F32), pltpu.SemaphoreType.DMA((6,))],
        compiler_params=pltpu.CompilerParams(vmem_limit_bytes=12 * 2**20),
        name="unpack",
    )(turn, received)


def exchange(value, axes):
    return lax.all_to_all(value, axes, 0, 0)


def copies(value, count):
    return jnp.broadcast_to(value[None], (count,) + value.shape)


def per_device(basis, density):
    chunks = lax.axis_size(MODE)
    slabs = lax.axis_size(SPACE)
    planes, width_y, width_z = basis.shape[2:]
    own = width_z // chunks
    scale = 1.0 / (3.0 * planes * width_y * width_z * slabs)
    turn = lax.axis_index("yh")
    chunk = lax.axis_index("x") * 2 + lax.abs(lax.axis_index("yl") - turn)
    density = lax.dynamic_slice_in_dim(density, chunk * own, own, axis=2)
    turn = turn.reshape(1)
    density = jnp.swapaxes(density.reshape(planes, width_y // 2, 2, own), 1, 2)
    density = density.reshape(planes, 2, width_y // 2 * own)
    root = jnp.sqrt(density)
    weights = jnp.stack([root, density * root])

    first = exchange(pack_first(turn, basis), MODE)
    second = exchange(pack_second(turn, basis), MODE)
    half = slabs // lax.axis_size("yh")
    route = [
        (mode * slabs + slab, (mode ^ (slab % half == 0)) * slabs + slab - 1)
        for mode in range(chunks)
        for slab in range(1, slabs)
    ]
    above = lax.ppermute(first, MODE + SPACE, route)
    part, faces = gram(0, scale, (first, second, weights))
    (part,) = gram(1, scale, (faces, above, weights, part))

    plane_axes = ("yh", "yl", "x")
    wide, deep = lax.axis_size(plane_axes), lax.axis_size("z")
    piece = exchange(part.reshape(wide, 384 // wide, 128), plane_axes).sum(0)
    piece = piece + lax.ppermute(piece, "core", [(0, 1), (1, 0)])
    piece = exchange(copies(piece, deep), "z").sum(0)
    packed = exchange(copies(piece, wide), plane_axes)

    send, inverse = solve(packed, first, second)
    rotated = unpack(turn, exchange(send, MODE)).reshape(basis.shape)
    high = lax.Precision.HIGHEST
    packed = packed.reshape(384, 128)
    stiff = jnp.concatenate([packed[:192], packed[192:, :64]], axis=1)
    stiff = jnp.tril(stiff) + jnp.tril(stiff, -1).T
    reduced = jnp.dot(jnp.dot(inverse, stiff, precision=high), inverse.T, precision=high)
    return rotated, reduced


def solution(mesh):
    modes, slabs = mesh.devices.shape
    half = 2 if slabs % 4 == 0 else 1
    inner = Mesh(mesh.devices.reshape(modes // 2, 2, half, slabs // half // 2, 2), MODE + SPACE)
    field = P(MODE, None, SPACE, None, None)
    return jax.shard_map(
        per_device,
        mesh=inner,
        in_specs=(field, P(SPACE, None, None)),
        out_specs=(field, P()),
        check_vma=False,
    )
```

```python
import functools
import math

import jax
import jax.numpy as jnp
import numpy as np
from jax import lax
from jax.experimental import pallas as pl
from jax.experimental.pallas import tpu as pltpu
from jax.sharding import Mesh, PartitionSpec as P

VMEM = pltpu.VMEM
MODE = ("x", "yl")
TURNED = ("yl", "x")
SPACE = ("yh", "z", "core")
F32 = jnp.float32
BF16 = jnp.bfloat16


def hex_matrices():
    poisson = 0.3
    lame_first = poisson / ((1.0 + poisson) * (1.0 - 2.0 * poisson))
    shear = 1.0 / (2.0 * (1.0 + poisson))
    elastic = np.zeros((6, 6))
    elastic[:3, :3] = lame_first
    for number in range(3):
        elastic[number, number] += 2.0 * shear
        elastic[number + 3, number + 3] = shear
    points = [0.5 - 0.5 / math.sqrt(3.0), 0.5 + 0.5 / math.sqrt(3.0)]
    corners = [(a, b, c) for a in (0, 1) for b in (0, 1) for c in (0, 1)]
    stiff = np.zeros((24, 24))
    for point_x in points:
        for point_y in points:
            for point_z in points:
                strain = np.zeros((6, 24))
                for number, corner in enumerate(corners):
                    shape_x = point_x if corner[0] else 1.0 - point_x
                    shape_y = point_y if corner[1] else 1.0 - point_y
                    shape_z = point_z if corner[2] else 1.0 - point_z
                    deriv_x = (2.0 * corner[0] - 1.0) * shape_y * shape_z
                    deriv_y = shape_x * (2.0 * corner[1] - 1.0) * shape_z
                    deriv_z = shape_x * shape_y * (2.0 * corner[2] - 1.0)
                    strain[0, 3 * number] = deriv_x
                    strain[1, 3 * number + 1] = deriv_y
                    strain[2, 3 * number + 2] = deriv_z
                    strain[3, 3 * number] = deriv_y
                    strain[3, 3 * number + 1] = deriv_x
                    strain[4, 3 * number + 1] = deriv_z
                    strain[4, 3 * number + 2] = deriv_y
                    strain[5, 3 * number] = deriv_z
                    strain[5, 3 * number + 2] = deriv_x
                stiff += strain.T @ elastic @ strain / 8.0
    line = np.array([[1.0 / 3.0, 1.0 / 6.0], [1.0 / 6.0, 1.0 / 3.0]])
    mass = np.kron(np.kron(line, line), line)
    return stiff, mass


def factors():
    stiff, mass = hex_matrices()
    pair = np.array([[1.0, 1.0], [-1.0, 1.0]])
    modes = np.kron(np.kron(pair, pair), pair)
    mass_weight = np.sqrt(np.diag(modes @ mass @ modes.T) / 64.0)
    both = np.kron(modes, np.eye(3))
    blocks = both @ stiff @ both.T / 64.0
    rows = []
    for label in range(8):
        index = [(label ^ (4 >> comp)) * 3 + comp for comp in range(3)]
        block = blocks[np.ix_(index, index)].copy()
        for k in range(3):
            if block[k, k] > 1e-9:
                row = block[k] / math.sqrt(block[k, k])
                rows.append([(index[b], float(row[b])) for b in range(3) if abs(row[b]) > 1e-9])
                block -= np.outer(row, row)
        assert np.abs(block).max() < 1e-9
    return mass_weight, rows


def swap_blocks(vectors):
    block = lax.broadcasted_iota(jnp.int32, vectors[0].shape, 1) // 16
    vectors = [pltpu.roll(v, 16 * k, 1) if k else v for k, v in enumerate(vectors)]
    for step in (1, 2, 4):
        moved = (block & step) != 0
        vectors = [jnp.where(moved, vectors[(k + step) % 8], vectors[k]) for k in range(8)]
    return [pltpu.roll(vectors[-k % 8], 128 - 16 * k, 1) if k else vectors[0] for k in range(8)]


def slot_of(comp, half):
    return comp * 2 + half


def edge_lane(plane, comp, half):
    return half * 6 + plane * 3 + comp


def turned(chunk, turn):
    return chunk // 2 + (4 * turn if chunk % 2 == 0 else 4 - 4 * turn)


def place_lines(lines, comp, turn, out_ref):
    for half in range(2):
        parts = swap_blocks([lines[2 * k + half] for k in range(8)])
        for chunk in range(8):
            out_ref[turned(chunk, turn), slot_of(comp, half)] = parts[chunk]


def pack_first_body(turn_ref, x_ref, out_ref, held_ref, sems):
    turn = turn_ref[0]
    copies_in = []
    for part in range(6):
        rows = pl.ds((part % 3 * 2 + part // 3) * 16, 16)
        copies_in.append(
            pltpu.make_async_copy(x_ref.at[:, rows, :], held_ref.at[part], sems.at[part])
        )
        copies_in[part].start()
    within = lax.broadcasted_iota(jnp.int32, (24, 128), 1) % 16
    edges = [jnp.zeros((24, 128), F32)] * 8
    for plane in range(2):
        for comp in range(3):
            copies_in[plane * 3 + comp].wait()
            lines = jnp.swapaxes(held_ref[plane * 3 + comp], 0, 1)
            for half in range(2):
                lane = edge_lane(plane, comp, half)
                for k in range(8):
                    value = lines[2 * k + half]
                    value = pltpu.roll(value, lane, 1) if lane else value
                    edges[k] = jnp.where(within == lane, value, edges[k])
            if plane == 0:
                place_lines(lines, comp, turn, out_ref)
    edges = swap_blocks(edges)
    for chunk in range(8):
        out_ref[turned(chunk, turn), 6] = edges[(chunk + 1) % 8]


def pack_first(turn, basis):
    return pl.pallas_call(
        pack_first_body,
        out_shape=jax.ShapeDtypeStruct((8, 7, 24, 128), F32),
        in_specs=[pl.BlockSpec(memory_space=pltpu.SMEM), pl.BlockSpec(memory_space=pl.ANY)],
        out_specs=pl.BlockSpec(memory_space=VMEM),
        scratch_shapes=[VMEM((6, 24, 16, 128), F32), pltpu.SemaphoreType.DMA((6,))],
        compiler_params=pltpu.CompilerParams(vmem_limit_bytes=60 * 2**20),
        name="pack_first",
    )(turn, basis.reshape(24, 96, 128))


def pack_second_body(turn_ref, x_ref, out_ref):
    for comp in range(3):
        first = (comp * 2 + 1) * 16
        lines = jnp.swapaxes(x_ref[:, first : first + 16, :], 0, 1)
        place_lines(lines, comp, turn_ref[0], out_ref)


def pack_second(turn, basis):
    return pl.pallas_call(
        pack_second_body,
        out_shape=jax.ShapeDtypeStruct((8, 6, 24, 128), F32),
        in_specs=[pl.BlockSpec(memory_space=pltpu.SMEM), pl.BlockSpec(memory_space=VMEM)],
        out_specs=pl.BlockSpec(memory_space=VMEM),
        compiler_params=pltpu.CompilerParams(vmem_limit_bytes=12 * 2**20),
        name="pack_second",
    )(turn, basis.reshape(24, 96, 128))


def gram_body(scale, layer, first_ref, second_ref, w_ref, *rest):
    if layer == 0:
        before_ref = None
        out_ref, faces_ref, mass_ref, stiff_ref = rest
        places = ((0, first_ref, first_ref, 0), (1, second_ref, first_ref, 1))
    else:
        before_ref, out_ref, mass_ref, stiff_ref = rest
        faces_ref = first_ref
        places = ((1, second_ref, second_ref, 0),)
    mass_weight, stiff_rows = factors()
    columns = 192
    last = lax.broadcasted_iota(jnp.int32, (16, 128), 1) % 16 == 15

    def read(ref, q, g, slot):
        parts = []
        for n in (2 * g, 2 * g + 1):
            t = n % 3
            parts.append(ref[n // 3 * 4 + q, slot, 8 * t : 8 * t + 8, :])
        return jnp.concatenate(parts, axis=0)

    def step(q, carry):
        for g in range(3):
            modes = {}
            start = pl.multiple_of(q * 48 + g * 16, 16)
            edges = {a: read(edge, q, g, 6) for a, _, edge, _ in places}
            for comp in range(3):
                faces = {}
                for a, ref, _, plane in places:
                    lines = {}
                    for half in range(2):
                        here = read(ref, q, g, slot_of(comp, half))
                        edge = pltpu.roll(edges[a], 15 - edge_lane(plane, comp, half), 1)
                        there = jnp.where(last, edge, pltpu.roll(here, 127, 1))
                        lines[half, 0] = here + there
                        lines[half, 1] = there - here
                    for pc in range(2):
                        even, odd = lines[0, pc], lines[1, pc]
                        following = pltpu.roll(even, 112, 1)
                        faces[a, 0, 0, pc] = odd + even
                        faces[a, 0, 1, pc] = odd - even
                        faces[a, 1, 0, pc] = following + odd
                        faces[a, 1, 1, pc] = following - odd
                for half in range(2):
                    for pb in range(2):
                        for pc in range(2):
                            slot = (half * 4 + pb * 2 + pc) * 3 + comp
                            if layer == 0:
                                faces_ref[slot, pl.ds(start, 16), :] = faces[1, half, pb, pc]
                            else:
                                faces[0, half, pb, pc] = faces_ref[slot, pl.ds(start, 16), :]
                for half in range(2):
                    for pb in range(2):
                        for pc in range(2):
                            low, high = faces[0, half, pb, pc], faces[1, half, pb, pc]
                            modes[half, (2 * pb + pc) * 3 + comp] = high + low
                            modes[half, (4 + 2 * pb + pc) * 3 + comp] = high - low
            def put(ref, slot, value):
                high = value.astype(BF16)
                low = (value - high.astype(F32)).astype(BF16)
                ref[pl.ds(start, 16), slot * 128 : slot * 128 + 128] = high
                ref[pl.ds(columns + start, 16), slot * 128 : slot * 128 + 128] = low

            for half in range(2):
                root = w_ref[0, layer, pl.ds(half, 1), :]
                cubed = w_ref[1, layer, pl.ds(half, 1), :]
                for mode in range(24):
                    value = modes[half, mode] * (root * float(mass_weight[mode // 3]))
                    put(mass_ref, 24 * half + mode, value)
                for number, row in enumerate(stiff_rows):
                    total = None
                    for mode, coef in row:
                        term = modes[half, mode] * (cubed * coef)
                        total = term if total is None else total + term
                    put(stiff_ref, len(stiff_rows) * half + number, total)
        return carry

    lax.fori_loop(0, 4, step, 0)

    def halves(ref):
        both = lax.dot_general(
            ref[...], ref[:columns, :], (((1,), (1,)), ((), ())), preferred_element_type=F32
        )
        return both[:columns, :] + both[columns:, :], both[columns:, :]

    mass, mass_cross = halves(mass_ref)
    stiff, stiff_cross = halves(stiff_ref)
    row = lax.broadcasted_iota(jnp.int32, (columns, columns), 0)
    col = lax.broadcasted_iota(jnp.int32, (columns, columns), 1)
    cross = jnp.where(row <= col, stiff_cross, mass_cross)
    mixed = (jnp.where(row >= col, stiff, mass) + cross.T) * scale
    diagonal = jnp.where(row == col, mass + mass_cross, 0.0)
    diagonal = jnp.sum(diagonal, axis=1, keepdims=True) * scale
    out_ref[:columns, :] = mixed[:, :128]
    out_ref[columns:, :64] = mixed[:, 128:]
    out_ref[columns:, 64:] = jnp.broadcast_to(diagonal, (columns, 64))
    if before_ref is not None:
        out_ref[...] += before_ref[...]


def gram(layer, scale, operands):
    stiff = len(factors()[1])
    shapes = [jax.ShapeDtypeStruct((384, 128), F32)]
    if layer == 0:
        shapes.append(jax.ShapeDtypeStruct((24, 192, 128), F32))
    return pl.pallas_call(
        functools.partial(gram_body, scale, layer),
        out_shape=shapes,
        in_specs=[pl.BlockSpec(memory_space=VMEM)] * len(operands),
        out_specs=[pl.BlockSpec(memory_space=VMEM)] * len(shapes),
        scratch_shapes=[
            VMEM((384, 2 * 24 * 128), BF16),
            VMEM((384, 2 * stiff * 128), BF16),
        ],
        compiler_params=pltpu.CompilerParams(vmem_limit_bytes=20 * 2**20),
        cost_estimate=pl.CostEstimate(flops=3 * 10**9, bytes_accessed=3 * 10**6, transcendentals=0),
        name="gram",
    )(*operands)


def dot32(a, b, contract=((1,), (0,))):
    return lax.dot_general(
        a, b, (contract, ((), ())), precision=lax.Precision.HIGHEST, preferred_element_type=F32
    )


def eliminate(block, first, size):
    groups = size // 8
    sub = lax.broadcasted_iota(jnp.int32, (8, 128), 0)
    lane = lax.broadcasted_iota(jnp.int32, (8, 128), 1)
    spread = {}
    for k in range(size):
        for t in range(k // 8, groups):
            tile = (first + k) // 128 * 128
            index = jnp.full((8, 128), first + k - tile, jnp.int32)
            spread[k, t] = jnp.take_along_axis(
                block[8 * t : 8 * t + 8, tile : tile + 128], index, axis=1
            )
    right = [jnp.where(lane == sub + 8 * t, 1.0, 0.0).astype(F32) for t in range(groups)]
    for i in range(size):
        at, inner = i // 8, i % 8
        inverse = 1.0 / spread[i, at][inner : inner + 1, :]
        factor = {t: spread[i, t] * inverse for t in range(at, groups)}
        factor[at] = jnp.where(sub > inner, factor[at], 0.0)
        for k in range(i + 1, size):
            entry = spread[i, k // 8][k % 8 : k % 8 + 1, :]
            for t in range(k // 8, groups):
                spread[k, t] = spread[k, t] - factor[t] * entry
        line = right[at][inner : inner + 1, :]
        for t in range(at, groups):
            right[t] = right[t] - factor[t] * line
    for t in range(groups):
        pivots = spread[8 * t, t]
        for inner in range(1, 8):
            pivots = jnp.where(sub == inner, spread[8 * t + inner, t], pivots)
        root = lax.rsqrt(pivots)
        right[t] = right[t] * (root * (1.5 - 0.5 * pivots * root * root))
    return jnp.concatenate(right, axis=0)[:, :size]


def split(value):
    high = value.astype(BF16)
    return high, (value - high.astype(F32)).astype(BF16)


def solve_body(g_ref, r0_ref, r1_ref, send_ref, inverse_ref, held_ref, sems):
    copies_out = []
    columns, size = 192, 32
    packed = g_ref[...].reshape(384, 128)
    mixed = jnp.concatenate([packed[:columns], packed[columns:, :64]], axis=1)
    diagonal = packed[columns:, 64:65]
    row = lax.broadcasted_iota(jnp.int32, (columns, columns), 0)
    col = lax.broadcasted_iota(jnp.int32, (columns, columns), 1)
    other = mixed.T
    mass = jnp.where(row < col, mixed, jnp.where(row == col, diagonal, other))
    unit = jnp.where(row == col, 1.0, 0.0).astype(F32)
    count = columns // size
    mass = jnp.concatenate([mass, jnp.zeros((columns, 64), F32)], axis=1)
    left = [mass[k * size : k * size + size] for k in range(count)]
    right = [unit[k * size : k * size + size] for k in range(count)]
    done = []
    for k in range(count):
        root = eliminate(left[k], k * size, size)
        line = dot32(root, left[k])
        if k + 1 < count:
            turned_line = line.T
            left[k + 1] = left[k + 1] - dot32(turned_line[(k + 1) * size : (k + 2) * size], line)
        ready = dot32(root, right[k])
        done.append(ready)
        if k + 1 < count:
            both = dot32(turned_line[(k + 1) * size :], ready)
            for i in range(k + 1, count):
                right[i] = right[i] - both[(i - k - 1) * size : (i - k) * size]
        if k + 2 < count:
            both = dot32(turned_line[(k + 2) * size :], line)
            for i in range(k + 2, count):
                left[i] = left[i] - both[(i - k - 2) * size : (i - k - 1) * size]
    inverse = jnp.concatenate(done, axis=0)
    inverse_ref[...] = inverse
    left_high, left_low = split(inverse)
    for plane, ref in enumerate((r0_ref, r1_ref)):
        for comp in range(3):
            sides = [
                jnp.concatenate([ref[m % 2 * 4 + m // 2, slot_of(comp, half)] for m in range(8)])
                for half in range(2)
            ]
            right_high, right_low = split(jnp.concatenate(sides, axis=1))
            total = jnp.dot(left_high, right_high, preferred_element_type=F32)
            total += jnp.dot(left_high, right_low, preferred_element_type=F32)
            total += jnp.dot(left_low, right_high, preferred_element_type=F32)
            for half in range(2):
                part = total[:, 128 * half : 128 * half + 128].reshape(8, 24, 128)
                for m in range(8):
                    held_ref[plane * 3 + comp, m % 2 * 4 + m // 2, half] = part[m]
            at = plane * 3 + comp
            target = send_ref.at[:, pl.ds(2 * at, 2)]
            copies_out.append(pltpu.make_async_copy(held_ref.at[at], target, sems.at[at]))
            copies_out[at].start()
    for copy in copies_out:
        copy.wait()


def solve(packed, first, second):
    return pl.pallas_call(
        solve_body,
        out_shape=(
            jax.ShapeDtypeStruct((8, 12, 24, 128), F32),
            jax.ShapeDtypeStruct((192, 192), F32),
        ),
        in_specs=[pl.BlockSpec(memory_space=VMEM)] * 3,
        out_specs=[pl.BlockSpec(memory_space=pl.ANY), pl.BlockSpec(memory_space=VMEM)],
        scratch_shapes=[VMEM((6, 8, 2, 24, 128), F32), pltpu.SemaphoreType.DMA((6,))],
        compiler_params=pltpu.CompilerParams(vmem_limit_bytes=20 * 2**20),
        name="solve",
    )(packed, first, second)


def unpack_body(turn_ref, t_ref, out_ref, held_ref, sems):
    turn = turn_ref[0]
    copies_out = []
    for plane in range(2):
        for comp in range(3):
            lines = [None] * 16
            for half in range(2):
                slot = plane * 6 + slot_of(comp, half)
                lines[half::2] = swap_blocks([t_ref[turned(chunk, turn), slot] for chunk in range(8)])
            part = plane * 3 + comp
            held_ref[part] = jnp.swapaxes(jnp.stack(lines), 0, 1)
            rows = pl.ds((comp * 2 + plane) * 16, 16)
            copies_out.append(
                pltpu.make_async_copy(held_ref.at[part], out_ref.at[:, rows, :], sems.at[part])
            )
            copies_out[part].start()
    for copy in copies_out:
        copy.wait()


def unpack(turn, received):
    return pl.pallas_call(
        unpack_body,
        out_shape=jax.ShapeDtypeStruct((24, 96, 128), F32),
        in_specs=[pl.BlockSpec(memory_space=pltpu.SMEM), pl.BlockSpec(memory_space=VMEM)],
        out_specs=pl.BlockSpec(memory_space=pl.ANY),
        scratch_shapes=[VMEM((6, 24, 16, 128), F32), pltpu.SemaphoreType.DMA((6,))],
        compiler_params=pltpu.CompilerParams(vmem_limit_bytes=12 * 2**20),
        name="unpack",
    )(turn, received)


def exchange(value, axes):
    return lax.all_to_all(value, axes, 0, 0)


def copies(value, count):
    return jnp.broadcast_to(value[None], (count,) + value.shape)


def per_device(basis, density):
    chunks = lax.axis_size(MODE)
    slabs = lax.axis_size(SPACE)
    planes, width_y, width_z = basis.shape[2:]
    own = width_z // chunks
    scale = 1.0 / (3.0 * planes * width_y * width_z * slabs)
    turn = lax.axis_index("yh")
    chunk = lax.axis_index("x") * 2 + lax.abs(lax.axis_index("yl") - turn)
    density = lax.dynamic_slice_in_dim(density, chunk * own, own, axis=2)
    turn = turn.reshape(1)
    density = jnp.swapaxes(density.reshape(planes, width_y // 2, 2, own), 1, 2)
    density = density.reshape(planes, 2, width_y // 2 * own)
    root = jnp.sqrt(density)
    weights = jnp.stack([root, density * root])

    first = exchange(pack_first(turn, basis), TURNED)
    second = exchange(pack_second(turn, basis), TURNED)
    half = slabs // lax.axis_size("yh")
    route = [
        (mode * slabs + slab, (mode ^ (slab % half == 0)) * slabs + slab - 1)
        for mode in range(chunks)
        for slab in range(1, slabs)
    ]
    above = lax.ppermute(first, MODE + SPACE, route)
    part, faces = gram(0, scale, (first, second, weights))
    (part,) = gram(1, scale, (faces, above, weights, part))

    plane_axes = ("yh", "yl", "x")
    wide, deep = lax.axis_size(plane_axes), lax.axis_size("z")
    piece = exchange(part.reshape(wide, 384 // wide, 128), plane_axes).sum(0)
    piece = piece + lax.ppermute(piece, "core", [(0, 1), (1, 0)])
    piece = exchange(copies(piece, deep), "z").sum(0)
    packed = exchange(copies(piece, wide), plane_axes)

    send, inverse = solve(packed, first, second)
    rotated = unpack(turn, exchange(send, TURNED)).reshape(basis.shape)
    high = lax.Precision.HIGHEST
    packed = packed.reshape(384, 128)
    stiff = jnp.concatenate([packed[:192], packed[192:, :64]], axis=1)
    stiff = jnp.tril(stiff) + jnp.tril(stiff, -1).T
    reduced = jnp.dot(jnp.dot(inverse, stiff, precision=high), inverse.T, precision=high)
    return rotated, reduced


def solution(mesh):
    modes, slabs = mesh.devices.shape
    half = 2 if slabs % 4 == 0 else 1
    inner = Mesh(mesh.devices.reshape(modes // 2, 2, half, slabs // half // 2, 2), MODE + SPACE)
    field = P(MODE, None, SPACE, None, None)
    return jax.shard_map(
        per_device,
        mesh=inner,
        in_specs=(field, P(SPACE, None, None)),
        out_specs=(field, P()),
        check_vma=False,
    )
```
